512 devices in a mesh: dp: 8 (over z_lo, core), head: 64 (over z_hi, x, y).
Axes of the slice: x: 4, y: 4, z: 16 (z_hi: 4, z_lo: 4; z = z_hi * 4 + z_lo), core: 2. Of those that a mesh axis runs over, the one named last changes fastest.
Arguments:
- queries: bfloat16 [32, 2, 128, 128], P('dp', None, 'head')
- cache_keys: bfloat16 [32, 1024, 64, 128], P('dp', None, 'head'), as said below
- cache_values: bfloat16 [32, 1024, 64, 128], P('dp', None, 'head'), as said below
- new_keys: bfloat16 [32, 2, 64, 128], P('dp', None, 'head'), as said below
- new_values: bfloat16 [32, 2, 64, 128], P('dp', None, 'head'), as said below
- key_index: int32 [64, 128], P('head'), may hold values from 0 to 15, as said below
- value_index: int32 [64, 128], P('head'), may hold values from 0 to 15, as said below
- scale_table: float32 [16], replicated, may hold values from 0.25 to 2
- lengths: int32 [32], P('dp'), may hold values from 1 to 1024, as said below
- head_mix: float32 [128, 128], replicated, may hold values from -0.5 to 0.5
- channel_mix: float32 [128, 128], replicated, may hold values from -0.5 to 0.5
- out_weight: bfloat16 [16384, 16384], P('head', 'dp'), may hold values from -0.046875 to 0.046875
- residual: bfloat16 [64, 16384], P(None, ('dp', 'head')), may hold values from -6 to 6
Outputs:
- layer_out: bfloat16 [64, 16384], P(None, ('dp', 'head'))
The draws below stay inside these ranges and needn't reach their ends.
Inputs may be any that keep to these rules, and one draw needn't show every extreme that they name: `lengths`: sequence 0 uses its whole cache. `cache_keys`: copies c and c2 are equal where c * 8 // 64 == c2 * 8 // 64. `cache_values`: copied likewise. `new_keys`: copied likewise. `new_values`: copied likewise. `key_index`: copied likewise. `value_index`: copied likewise.
All inputs are finite; a program needn't handle non-finite values.
Results may differ from the reference program's by a relative error of at most 0.0056.
The reference program's roundings to bfloat16 on the way count: a program that leaves them out, or rounds other values in their place, can miss the bound.
Values may be sent and summed in bfloat16 or wider, within the bound.
A program may use at most 64 MiB of HBM per device.

```python
import math
import jax
import jax.numpy as jnp
from jax import lax

HD = 128
KV_HEADS = 8
HEAD_DEV = 2
STEPS = 2
CACHE = 1024
LEVELS = 16
SEQS = 32
HEADS = 128
KV_COPIES = 64
D = 16384
TOKENS = 64


def copied(drawn):
    return jnp.repeat(drawn, KV_COPIES // KV_HEADS, axis=-2)


def normal_heads(key, rows):
    drawn = jax.random.normal(key, (SEQS, rows, KV_HEADS, HD), jnp.float32)
    return copied(jnp.clip(drawn, -6.0, 6.0).astype(jnp.bfloat16))


def draw_queries(key, part):
    key = jax.random.fold_in(key, 11)
    base = jax.random.normal(key, (SEQS, STEPS, HEADS, HD), jnp.float32)
    return base.astype(jnp.bfloat16)


def draw_cache_keys(key, part):
    key = jax.random.fold_in(key, 31)
    return normal_heads(key, CACHE)


def draw_cache_values(key, part):
    key = jax.random.fold_in(key, 37)
    return normal_heads(key, CACHE)


def draw_new_keys(key, part):
    key = jax.random.fold_in(key, 41)
    return normal_heads(key, STEPS)


def draw_new_values(key, part):
    key = jax.random.fold_in(key, 43)
    return normal_heads(key, STEPS)


def draw_key_index(key, part):
    key = jax.random.fold_in(key, 47)
    return copied(jax.random.randint(key, (KV_HEADS, 1, HD), 0, LEVELS)).reshape(KV_COPIES, HD).astype(jnp.int32)


def draw_value_index(key, part):
    key = jax.random.fold_in(key, 53)
    return copied(jax.random.randint(key, (KV_HEADS, 1, HD), 0, LEVELS)).reshape(KV_COPIES, HD).astype(jnp.int32)


def draw_lengths(key, part):
    key = jax.random.fold_in(key, 23)
    drawn = jax.random.randint(key, (SEQS,), 1, CACHE + 1)
    return jnp.where(jnp.arange(SEQS) == 0, CACHE, drawn).astype(jnp.int32)


def levels(stream_key, shape, cuts, smallest, high):
    def one(position, shards_of):
        draws = jax.random.uniform(jax.random.fold_in(jax.random.fold_in(stream_key, 6), position), (shards_of,), jnp.float32, smallest / len(cuts), high / len(cuts))
        return jnp.repeat(jnp.exp(draws), shape[position] // shards_of).reshape((-1,) + (1,) * (len(shape) - position - 1))

    level = one(*cuts[0])
    for cut in cuts[1:]:
        level = level * one(*cut)
    return level


def noise(rng, shape, deviation, limit, shards=(), held_as=jnp.bfloat16):
    values = deviation * jax.random.normal(rng, shape, jnp.float32)
    if shards:
        values = values * levels(rng, shape, shards, -0.22, 0.18)
    return jnp.clip(values, -limit, limit).astype(held_as)


def setup_inputs(seed: int = 0) -> dict:
    arg_keys = jax.random.split(jax.random.key(seed), 14)
    queries = draw_queries(jax.random.fold_in(arg_keys[13], 71), 0)
    cache_keys = draw_cache_keys(jax.random.fold_in(arg_keys[13], 71), 0)
    cache_values = draw_cache_values(jax.random.fold_in(arg_keys[13], 71), 0)
    new_keys = draw_new_keys(jax.random.fold_in(arg_keys[13], 71), 0)
    new_values = draw_new_values(jax.random.fold_in(arg_keys[13], 71), 0)
    key_index = draw_key_index(jax.random.fold_in(arg_keys[13], 71), 0)
    value_index = draw_value_index(jax.random.fold_in(arg_keys[13], 71), 0)
    scale_table = jnp.clip(jnp.exp(jax.random.uniform(arg_keys[7], (LEVELS,), jnp.float32, math.log(0.25), math.log(2.0))), 0.25, 2.0)
    lengths = draw_lengths(jax.random.fold_in(arg_keys[13], 71), 0)
    head_mix = noise(arg_keys[9], (HEADS, HEADS), HEADS ** -0.5, 0.5, (), jnp.float32)
    channel_mix = noise(arg_keys[10], (HD, HD), HD ** -0.5, 0.5, (), jnp.float32)
    out_weight = noise(arg_keys[11], (D, D), D ** -0.5, 0.046875, ((0, 64), (1, 8)))
    residual = noise(arg_keys[12], (TOKENS, D), 1.0, 6.0, ((1, 512),))
    return {"queries": queries, "cache_keys": cache_keys, "cache_values": cache_values, "new_keys": new_keys, "new_values": new_values, "key_index": key_index, "value_index": value_index, "scale_table": scale_table, "lengths": lengths, "head_mix": head_mix, "channel_mix": channel_mix, "out_weight": out_weight, "residual": residual}


def one_sequence(query, keys, values, fresh_keys, fresh_values, length, key_scale, value_scale, head_mix, channel_mix):
    groups = HEADS // HEAD_DEV
    inverse = 1.0 / (HD ** 0.5)
    grouped = query.astype(jnp.float32).reshape(STEPS, groups, HEAD_DEV, HD)
    scaled = (grouped * key_scale[None, :, None, :]).astype(jnp.bfloat16)
    cache_score = jnp.einsum("tkgd,lkd->tkgl", scaled.astype(jnp.float32), keys.astype(jnp.float32)) * inverse
    valid = jnp.arange(CACHE) < length
    cache_score = jnp.where(valid[None, None, None, :], cache_score, -jnp.inf)
    new_score = jnp.einsum("tkgd,ukd->tkgu", grouped, fresh_keys.astype(jnp.float32)) * inverse
    causal = jnp.arange(STEPS)[:, None] >= jnp.arange(STEPS)[None, :]
    new_score = jnp.where(causal[:, None, None, :], new_score, -jnp.inf)
    top = jnp.maximum(jnp.max(cache_score, axis=-1), jnp.max(new_score, axis=-1))
    cache_exp = jnp.exp(cache_score - top[..., None])
    new_exp = jnp.exp(new_score - top[..., None])
    total = jnp.sum(cache_exp, axis=-1) + jnp.sum(new_exp, axis=-1)
    cache_weight = cache_exp.astype(jnp.bfloat16).astype(jnp.float32)
    new_weight = new_exp.astype(jnp.bfloat16).astype(jnp.float32)
    from_cache = jnp.einsum("tkgl,lkd->tkgd", cache_weight, values.astype(jnp.float32)) * value_scale[None, :, None, :]
    from_new = jnp.einsum("tkgu,ukd->tkgd", new_weight, fresh_values.astype(jnp.float32))
    attended = ((from_cache + from_new) / total[..., None]).reshape(STEPS, HEADS, HD)
    inner = jnp.einsum("thd,de->the", attended, channel_mix, precision=lax.Precision.HIGHEST)
    mixed = jnp.einsum("tge,gh->the", inner, head_mix, precision=lax.Precision.HIGHEST)
    return mixed.reshape(STEPS, D).astype(jnp.bfloat16)


def reference(queries, cache_keys, cache_values, new_keys, new_values, key_index, value_index, scale_table, lengths, head_mix, channel_mix, out_weight, residual):
    key_scale = scale_table[key_index]
    value_scale = scale_table[value_index]

    def per_item(items):
        return one_sequence(items[0], items[1], items[2], items[3], items[4], items[5], key_scale, value_scale, head_mix, channel_mix)

    mixed = lax.map(per_item, (queries, cache_keys, cache_values, new_keys, new_values, lengths))
    mixed = mixed.reshape(TOKENS, D)
    projected = jnp.dot(mixed, out_weight, preferred_element_type=jnp.float32)
    return (residual.astype(jnp.float32) + projected).astype(jnp.bfloat16)
```

```python
import functools

import jax
import jax.numpy as jnp
from jax import lax
from jax.experimental import pallas as pl
from jax.experimental.pallas import tpu as pltpu
from jax.sharding import PartitionSpec as P

MESH = pl.DeviceIdType.MESH
F32, BF16 = jnp.float32, jnp.bfloat16
DP, NZ, NP = 8, 4, 16
SEQ, STEPS, HEADS, HD, CACHE = 4, 2, 2, 128, 1024
ROWS = SEQ * STEPS
NT = (((1,), (1,)), ((), ()))


def split2(x):
    high = x.astype(BF16)
    return high, (x - high.astype(F32)).astype(BF16)


def dot(a, b):
    return jnp.dot(a, b, preferred_element_type=F32)


def dot_nt(a, b):
    return lax.dot_general(a, b, NT, preferred_element_type=F32)


def kernel(
    q_hbm, k_hbm, v_hbm, nk_hbm, nv_hbm, ki_hbm, vi_hbm, tab_hbm, len_hbm, hm_hbm, cm_hbm, w_hbm, res_hbm,
    out_ref,
    q_v, k_v, v_v, nk_v, nv_v, ki_v, vi_v, tab_s, len_s, hm_v, cm_v, w_v, res_v,
    wt, kron, z_buf, p_send, p_buf, d_send, d_buf, o_send, o_buf, f_send, f_buf,
    in_sem, k_sem, v_sem,
    z_ss, z_rs, p_ss, p_rs, d_ss, d_rs, o_ss, o_rs, f_ss, f_rs,
):
    j = lax.axis_index("dp")
    i = lax.axis_index("head")
    z = i // NP
    p = i % NP
    x = p // 4
    y = p % 4

    small = [
        (q_hbm, q_v), (ki_hbm, ki_v), (tab_hbm, tab_s), (len_hbm, len_s), (nk_hbm, nk_v), (nv_hbm, nv_v),
        (vi_hbm, vi_v), (hm_hbm, hm_v), (cm_hbm, cm_v), (res_hbm, res_v), (w_hbm, w_v),
    ]
    loads = [pltpu.make_async_copy(a, b, in_sem.at[n]) for n, (a, b) in enumerate(small)]
    k_loads = [pltpu.make_async_copy(k_hbm.at[s], k_v.at[s], k_sem.at[s]) for s in range(SEQ)]
    v_loads = [pltpu.make_async_copy(v_hbm.at[s], v_v.at[s], v_sem.at[s]) for s in range(SEQ)]
    for c in loads[:4]:
        c.start()
    for c in k_loads:
        c.start()
    for c in loads[4:-1]:
        c.start()
    for c in v_loads:
        c.start()
    loads[-1].start()

    barrier = pltpu.get_barrier_semaphore()

    def hello(device):
        pl.semaphore_signal(barrier, inc=1, device_id=device, device_id_type=MESH)

    for n in range(1, NZ):
        hello((j, (z + n) % NZ * NP + p))

    @pl.loop(1, NP)
    def _(n):
        hello((j, z * NP + (p + n) % NP))

    for n in range(1, DP):
        hello(((j + n) % DP, i))

    for c in loads[:-1]:
        c.wait()

    m_row = lax.broadcasted_iota(jnp.int32, (NP * 16, 128), 0)
    m_col = lax.broadcasted_iota(jnp.int32, (NP * 16, 128), 1)
    pick_h = (m_col == z * 32 + m_row // 8).astype(F32)
    g_row = lax.broadcasted_iota(jnp.int32, (128, NZ * 16), 0)
    g_col = lax.broadcasted_iota(jnp.int32, (128, NZ * 16), 1)
    pick_g = (g_row == g_col // 16 * 32 + p * 2 + g_col // 8 % 2).astype(F32)
    wide = lax.dot_general(pick_h, hm_v[...], NT, precision=lax.Precision.HIGHEST, preferred_element_type=F32)
    wide = jnp.dot(wide, pick_g, precision=lax.Precision.HIGHEST, preferred_element_type=F32)
    a_row = lax.broadcasted_iota(jnp.int32, (NP * 16, NZ * 16), 0)
    a_col = lax.broadcasted_iota(jnp.int32, (NP * 16, NZ * 16), 1)
    wide = jnp.where(a_row % 8 == a_col % 8, wide, 0.0)
    wide_h, wide_l = split2(wide)
    kron[:, 0:128] = jnp.concatenate([wide_h, wide_l], axis=1)
    kron[:, 128:256] = jnp.concatenate([wide_h, jnp.zeros_like(wide_h)], axis=1)
    c_h, c_l = split2(cm_v[...])
    chan = jnp.concatenate([c_h, c_l, c_h], axis=0)

    key_scale = jnp.zeros((1, HD), F32)
    value_scale = jnp.zeros((1, HD), F32)
    for n in range(16):
        key_scale = jnp.where(ki_v[...] == n, tab_s[n], key_scale)
        value_scale = jnp.where(vi_v[...] == n, tab_s[n], value_scale)
    q_all = q_v[...].astype(F32)
    q = jnp.concatenate(
        [q_all[s, t, h : h + 1, :] for h in range(HEADS) for s in range(SEQ) for t in range(STEPS)], axis=0
    )
    scaled = (q * key_scale).astype(BF16)
    q_b = q.astype(BF16)
    nk_all = nk_v[...].astype(F32)
    nv_all = nv_v[...].astype(F32)
    nk = jnp.concatenate([nk_all[s] for s in range(SEQ)], axis=0).astype(BF16)
    nv = jnp.concatenate([nv_all[s] for s in range(SEQ)], axis=0).astype(BF16)

    row = lax.broadcasted_iota(jnp.int32, (16, CACHE), 0)
    row_seq = row % 8 // 2
    score = jnp.zeros((16, CACHE), F32)
    length = jnp.zeros((16, CACHE), jnp.int32)
    for s in range(SEQ):
        k_loads[s].wait()
        score = jnp.where(row_seq == s, dot_nt(scaled, k_v[s]), score)
        length = jnp.where(row_seq == s, len_s[s], length)
    inverse = 1.0 / HD**0.5
    place = lax.broadcasted_iota(jnp.int32, (16, CACHE), 1)
    score = jnp.where(place < length, score * inverse, -jnp.inf)
    new_row = lax.broadcasted_iota(jnp.int32, (16, 8), 0)
    new_col = lax.broadcasted_iota(jnp.int32, (16, 8), 1)
    seen = (new_row % 8 // 2 == new_col // 2) & (new_col % 2 <= new_row % 2)
    new_score = jnp.where(seen, dot_nt(q_b, nk) * inverse, -jnp.inf)
    top = jnp.maximum(jnp.max(score, axis=1, keepdims=True), jnp.max(new_score, axis=1, keepdims=True))
    weight = jnp.exp(score - top)
    new_weight = jnp.exp(new_score - top)
    total = jnp.sum(weight, axis=1, keepdims=True) + jnp.sum(new_weight, axis=1, keepdims=True)
    weight = weight.astype(BF16)
    attended = jnp.zeros((16, HD), F32)
    for s in range(SEQ):
        v_loads[s].wait()
        attended = jnp.where(row_seq[:, :HD] == s, dot(weight, v_v[s]), attended)
    attended = (attended * value_scale + dot(new_weight.astype(BF16), nv)) / total
    a_h, a_l = split2(attended)
    inner = dot(jnp.concatenate([a_h, a_h, a_l], axis=1), chan)
    z_buf[z] = inner

    pl.semaphore_wait(barrier, NZ - 1 + NP - 1 + DP - 1)

    def z_copy(n):
        return pltpu.make_async_remote_copy(
            z_buf.at[z], z_buf.at[z], z_ss.at[n], z_rs.at[n], (j, (z + n) % NZ * NP + p), MESH
        )

    for n in range(1, NZ):
        z_copy(n).start()

    loads[-1].wait()

    @pl.loop(0, 16)
    def _(t):
        turned = w_v[:, pl.ds(pl.multiple_of(t * 128, 128), 128)].astype(F32).T.astype(BF16)
        for n in range(8):
            start = pl.multiple_of((t % 4 * 4 + n // 2) * 64 + t // 4 * 16, 16)
            wt[pl.ds(start, 16), n % 2 * 256 : n % 2 * 256 + 256] = turned[n * 16 : n * 16 + 16, :]

    for n in range(1, NZ):
        z_copy(n).wait_recv()

    held_h, held_l = split2(z_buf[...].reshape(NZ * 16, HD))
    held = jnp.concatenate([held_h, held_h, held_l, jnp.zeros_like(held_l)], axis=0)
    p_send[...] = dot(kron[...], held).astype(BF16).reshape(NP, 16, HD)

    def p_copy(n):
        to = (p + n) % NP
        return pltpu.make_async_remote_copy(
            p_send.at[to], p_buf.at[p], p_ss.at[n], p_rs.at[n], (j, z * NP + to), MESH
        )

    @pl.loop(1, NP)
    def _(n):
        p_copy(n).start()

    def p_take(n, total):
        p_copy(n).wait_recv()
        return total + p_buf[(p + NP - n) % NP].astype(F32)

    mixed = lax.fori_loop(1, NP, p_take, p_send[p].astype(F32))

    d_send[...] = mixed.astype(BF16)

    def d_copy(n):
        return pltpu.make_async_remote_copy(
            d_send, d_buf.at[j], d_ss.at[n], d_rs.at[n], ((j + n) % DP, i), MESH
        )

    for n in range(1, DP):
        d_copy(n).start()
    d_buf[j] = d_send[...]
    for n in range(1, DP):
        d_copy(n).wait_recv()

    d_all = d_buf[...].astype(F32)
    rows = jnp.concatenate(
        [d_all[:, h * 8 : h * 8 + 8, :].reshape(DP * ROWS, HD).astype(BF16) for h in range(HEADS)], axis=1
    )
    none = jnp.zeros_like(rows)
    both = jnp.concatenate(
        [jnp.concatenate([rows, none], axis=1), jnp.concatenate([none, rows], axis=1)], axis=0
    )

    def o_copy(n, m):
        to = (x + n) % 4 * 4 + (y + m) % 4
        return pltpu.make_async_remote_copy(
            o_send.at[to], o_buf.at[p], o_ss.at[n * 4 + m], o_rs.at[n * 4 + m], (j, z * NP + to), MESH
        )

    for n in (2, 1, 3, 0):
        column = (x + n) % 4
        part = dot_nt(wt[pl.ds(pl.multiple_of(column * 256, 256), 256), :], both)
        o_send[pl.ds(column * 4, 4)] = part.astype(BF16).reshape(4, 64, 128)
        for m in (2, 1, 3, 0):
            if n or m:
                o_copy(n, m).start()

    summed = o_send[p].astype(F32)
    for n in (2, 1, 3, 0):
        for m in (2, 1, 3, 0):
            if n or m:
                o_copy(n, m).wait_recv()
                summed = summed + o_buf[(x + 4 - n) % 4 * 4 + (y + 4 - m) % 4].astype(F32)

    f_send[...] = summed.reshape(NZ, 16, 128)

    def f_copy(n):
        to = (z + n) % NZ
        return pltpu.make_async_remote_copy(
            f_send.at[to], f_buf.at[n], f_ss.at[n], f_rs.at[n], (j, to * NP + p), MESH
        )

    for n in range(1, NZ):
        f_copy(n).start()
    result = f_send[z]
    for n in range(1, NZ):
        f_copy(n).wait_recv()
        result = result + f_buf[n]
    result = jnp.concatenate([result[:, :64], result[:, 64:]], axis=0)
    out_ref[...] = (res_v[...].astype(F32) + result).astype(BF16)

    for n in range(1, NZ):
        z_copy(n).wait_send()

    @pl.loop(1, NP)
    def _(n):
        p_copy(n).wait_send()

    for n in range(1, DP):
        d_copy(n).wait_send()
    for n in range(4):
        for m in range(4):
            if n or m:
                o_copy(n, m).wait_send()
    for n in range(1, NZ):
        f_copy(n).wait_send()


def local(
    queries, cache_keys, cache_values, new_keys, new_values, key_index, value_index, scale_table, lengths,
    head_mix, channel_mix, out_weight, residual,
):
    vmem, dma = pltpu.VMEM, pltpu.SemaphoreType.DMA
    turned = pl.pallas_call(
        kernel,
        out_shape=jax.ShapeDtypeStruct((32, 64), BF16),
        in_specs=[pl.BlockSpec(memory_space=pl.ANY)] * 13,
        out_specs=pl.BlockSpec(memory_space=pltpu.VMEM),
        scratch_shapes=[
            vmem((SEQ, STEPS, HEADS, HD), BF16),
            vmem((SEQ, CACHE, HD), BF16),
            vmem((SEQ, CACHE, HD), BF16),
            vmem((SEQ, STEPS, HD), BF16),
            vmem((SEQ, STEPS, HD), BF16),
            vmem((1, HD), jnp.int32),
            vmem((1, HD), jnp.int32),
            pltpu.SMEM((16,), F32),
            pltpu.SMEM((SEQ,), jnp.int32),
            vmem((128, 128), F32),
            vmem((128, 128), F32),
            vmem((256, 2048), BF16),
            vmem((32, 64), BF16),
            vmem((1024, 512), BF16),
            vmem((256, 256), BF16),
            vmem((NZ, 16, HD), F32),
            vmem((NP, 16, HD), BF16),
            vmem((NP, 16, HD), BF16),
            vmem((16, HD), BF16),
            vmem((DP, 16, HD), BF16),
            vmem((NP, 64, 128), BF16),
            vmem((NP, 64, 128), BF16),
            vmem((NZ, 16, 128), F32),
            vmem((NZ, 16, 128), F32),
            dma((11,)),
            dma((SEQ,)),
            dma((SEQ,)),
            dma((NZ,)), dma((NZ,)),
            dma((NP,)), dma((NP,)),
            dma((DP,)), dma((DP,)),
            dma((NP,)), dma((NP,)),
            dma((NZ,)), dma((NZ,)),
        ],
        compiler_params=pltpu.CompilerParams(
            collective_id=0, has_side_effects=True, vmem_limit_bytes=48 * 1024 * 1024
        ),
    )(
        queries,
        cache_keys.reshape(SEQ, CACHE, HD),
        cache_values.reshape(SEQ, CACHE, HD),
        new_keys.reshape(SEQ, STEPS, HD),
        new_values.reshape(SEQ, STEPS, HD),
        key_index, value_index, scale_table, lengths, head_mix, channel_mix, out_weight, residual.T,
    )
    return turned.T


def solution(mesh):
    in_specs = (
        P("dp", None, "head", None),
        P("dp", None, "head", None),
        P("dp", None, "head", None),
        P("dp", None, "head", None),
        P("dp", None, "head", None),
        P("head", None),
        P("head", None),
        P(),
        P("dp"),
        P(),
        P(),
        P("head", "dp"),
        P(None, ("dp", "head")),
    )
    out_specs = P(None, ("dp", "head"))
    return jax.shard_map(local, mesh=mesh, in_specs=in_specs, out_specs=out_specs, check_vma=False)
```

```python
import functools

import jax
import jax.numpy as jnp
from jax import lax
from jax.experimental import pallas as pl
from jax.experimental.pallas import tpu as pltpu
from jax.sharding import PartitionSpec as P

MESH = pl.DeviceIdType.MESH
F32, BF16 = jnp.float32, jnp.bfloat16
DP, NZ, NP = 8, 4, 16
SEQ, STEPS, HEADS, HD, CACHE = 4, 2, 2, 128, 1024
ROWS = SEQ * STEPS
FAR = [(n, m) for n in (2, 1, 3, 0) for m in (2, 1, 3, 0) if n or m]
NEAR = sorted(FAR, key=lambda at: min(at[0], 4 - at[0]) + min(at[1], 4 - at[1]))
SLOTS = (2, 1, 3, 0)
NT = (((1,), (1,)), ((), ()))


def split2(x):
    high = x.astype(BF16)
    return high, (x - high.astype(F32)).astype(BF16)


def dot(a, b):
    return jnp.dot(a, b, preferred_element_type=F32)


def dot_nt(a, b):
    return lax.dot_general(a, b, NT, preferred_element_type=F32)


def kernel(
    q_hbm, k_hbm, v_hbm, nk_hbm, nv_hbm, ki_hbm, vi_hbm, tab_hbm, len_hbm, hm_hbm, cm_hbm, w_hbm, res_hbm,
    out_ref,
    q_v, k_v, v_v, nk_v, nv_v, ki_v, vi_v, tab_s, len_s, hm_v, cm_v, w_v, res_v,
    wt, kron, z_buf, p_send, p_buf, d_send, d_buf, o_send, o_buf, f_send, f_buf,
    in_sem, k_sem, v_sem,
    z_ss, z_rs, p_ss, p_rs, d_ss, d_rs, o_ss, o_rs, f_ss, f_rs,
):
    j = lax.axis_index("dp")
    i = lax.axis_index("head")
    z = i // NP
    p = i % NP
    x = p // 4
    y = p % 4

    barrier = pltpu.get_barrier_semaphore()

    def hello(device):
        pl.semaphore_signal(barrier, inc=1, device_id=device, device_id_type=MESH)

    late = z >= 2
    pair = z + 1 - 2 * (z % 2)
    facing = 3 - z
    across = (z + 2) % NZ
    hello((j, facing * NP + p))
    hello((j, pair * NP + p))

    @pl.when(z < 2)
    def _():
        hello((j, across * NP + p))

    for n in (2, 1, 3, 0):
        for m in (2, 1, 3, 0):
            if n or m:
                hello((j, z * NP + (x + n) % 4 * 4 + (y + m) % 4))
    for n in range(1, DP):
        hello(((j + n) % DP, i))

    small = [
        (hm_hbm, hm_v), (cm_hbm, cm_v), (q_hbm, q_v), (ki_hbm, ki_v), (tab_hbm, tab_s), (len_hbm, len_s),
        (nk_hbm, nk_v), (nv_hbm, nv_v), (vi_hbm, vi_v), (res_hbm, res_v), (w_hbm, w_v),
    ]
    loads = [pltpu.make_async_copy(a, b, in_sem.at[n]) for n, (a, b) in enumerate(small)]
    k_loads = [pltpu.make_async_copy(k_hbm.at[s], k_v.at[s], k_sem.at[s]) for s in range(SEQ)]
    v_loads = [pltpu.make_async_copy(v_hbm.at[s], v_v.at[s], v_sem.at[s]) for s in range(SEQ)]
    for c in loads[:-1]:
        c.start()
    for c in k_loads:
        c.start()
    for c in v_loads:
        c.start()
    loads[-1].start()

    for c in loads[:2]:
        c.wait()

    m_row = lax.broadcasted_iota(jnp.int32, (NP * 16, 128), 0)
    m_col = lax.broadcasted_iota(jnp.int32, (NP * 16, 128), 1)
    pick_h = (m_col == z * 32 + m_row // 8).astype(F32)
    g_row = lax.broadcasted_iota(jnp.int32, (128, NZ * 16), 0)
    g_col = lax.broadcasted_iota(jnp.int32, (128, NZ * 16), 1)
    pick_g = (g_row == g_col // 16 * 32 + p * 2 + g_col // 8 % 2).astype(F32)
    wide = lax.dot_general(pick_h, hm_v[...], NT, precision=lax.Precision.HIGHEST, preferred_element_type=F32)
    wide = jnp.dot(wide, pick_g, precision=lax.Precision.HIGHEST, preferred_element_type=F32)
    a_row = lax.broadcasted_iota(jnp.int32, (NP * 16, NZ * 16), 0)
    a_col = lax.broadcasted_iota(jnp.int32, (NP * 16, NZ * 16), 1)
    wide = jnp.where(a_row % 8 == a_col % 8, wide, 0.0)
    wide_h, wide_l = split2(wide)
    kron[...] = jnp.concatenate([wide_h, wide_l], axis=1)
    c_h, c_l = split2(cm_v[...])
    chan = jnp.concatenate([c_h, c_l, c_h], axis=0)

    for c in loads[2:-1]:
        c.wait()
    key_scale = jnp.zeros((1, HD), F32)
    value_scale = jnp.zeros((1, HD), F32)
    for n in range(16):
        key_scale = jnp.where(ki_v[...] == n, tab_s[n], key_scale)
        value_scale = jnp.where(vi_v[...] == n, tab_s[n], value_scale)
    q_all = q_v[...].astype(F32)
    q = jnp.concatenate(
        [q_all[s, t, h : h + 1, :] for h in range(HEADS) for s in range(SEQ) for t in range(STEPS)], axis=0
    )
    scaled = (q * key_scale).astype(BF16)
    q_b = q.astype(BF16)
    nk_all = nk_v[...].astype(F32)
    nv_all = nv_v[...].astype(F32)
    nk = jnp.concatenate([nk_all[s] for s in range(SEQ)], axis=0).astype(BF16)
    nv = jnp.concatenate([nv_all[s] for s in range(SEQ)], axis=0).astype(BF16)

    row = lax.broadcasted_iota(jnp.int32, (16, CACHE), 0)
    row_seq = row % 8 // 2
    score = jnp.zeros((16, CACHE), F32)
    length = jnp.zeros((16, CACHE), jnp.int32)
    for s in range(SEQ):
        k_loads[s].wait()
        score = jnp.where(row_seq == s, dot_nt(scaled, k_v[s]), score)
        length = jnp.where(row_seq == s, len_s[s], length)
    inverse = 1.0 / HD**0.5
    place = lax.broadcasted_iota(jnp.int32, (16, CACHE), 1)
    score = jnp.where(place < length, score * inverse, -jnp.inf)
    new_row = lax.broadcasted_iota(jnp.int32, (16, 8), 0)
    new_col = lax.broadcasted_iota(jnp.int32, (16, 8), 1)
    seen = (new_row % 8 // 2 == new_col // 2) & (new_col % 2 <= new_row % 2)
    new_score = jnp.where(seen, dot_nt(q_b, nk) * inverse, -jnp.inf)
    top = jnp.maximum(jnp.max(score, axis=1, keepdims=True), jnp.max(new_score, axis=1, keepdims=True))
    weight = jnp.exp(score - top)
    new_weight = jnp.exp(new_score - top)
    total = jnp.sum(weight, axis=1, keepdims=True) + jnp.sum(new_weight, axis=1, keepdims=True)
    weight = weight.astype(BF16)
    attended = jnp.zeros((16, HD), F32)
    for s in range(SEQ):
        v_loads[s].wait()
        attended = jnp.where(row_seq[:, :HD] == s, dot(weight, v_v[s]), attended)
    attended = (attended * value_scale + dot(new_weight.astype(BF16), nv)) / total
    a_h, a_l = split2(attended)
    inner = dot(jnp.concatenate([a_h, a_h, a_l], axis=1), chan)
    z_buf[z] = inner.astype(BF16)

    pl.semaphore_wait(barrier, NP - 1 + DP - 1 + 2 + z // 2)

    def z_copy(n, block, to):
        return pltpu.make_async_remote_copy(
            z_buf.at[block], z_buf.at[block], z_ss.at[n], z_rs.at[block], (j, to * NP + p), MESH
        )

    straight = z_copy(2, z, across)
    onward = z_copy(2, pair, facing)

    @pl.when(late)
    def _():
        straight.start()

    z_copy(0, z, facing).start()
    z_copy(1, z, pair).start()

    @pl.when(z < 2)
    def _():
        z_copy(1, pair, pair).wait_recv()
        onward.start()

    loads[-1].wait()
    for k, n in enumerate(SLOTS):
        first = (z + n) % NZ * 512

        @pl.loop(0, 4)
        def _(t, k=k, first=first):
            turned = w_v[:, pl.ds(pl.multiple_of(first + t * 128, 128), 128)].astype(F32).T.astype(BF16)
            for n in range(8):
                start = pl.multiple_of(k * 256 + (t * 4 + n // 2) * 16, 16)
                wt[pl.ds(start, 16), n % 2 * 256 : n % 2 * 256 + 256] = turned[n * 16 : n * 16 + 16, :]

    @pl.when(late)
    def _():
        z_copy(1, pair, pair).wait_recv()

    z_copy(0, facing, facing).wait_recv()
    z_copy(2, across, across).wait_recv()

    held = z_buf[...].reshape(NZ * 16, HD)
    p_send[...] = dot(kron[...], jnp.concatenate([held, held], axis=0)).astype(BF16).reshape(NP, 16, HD)

    def p_copy(n, m):
        to = (x + n) % 4 * 4 + (y + m) % 4
        return pltpu.make_async_remote_copy(
            p_send.at[to], p_buf.at[p], p_ss.at[n * 4 + m], p_rs.at[n * 4 + m], (j, z * NP + to), MESH
        )

    for n, m in FAR:
        p_copy(n, m).start()
    mixed = p_send[p].astype(F32)
    for n, m in NEAR:
        p_copy(n, m).wait_recv()
        mixed = mixed + p_buf[(x + 4 - n) % 4 * 4 + (y + 4 - m) % 4].astype(F32)

    d_send[...] = mixed.astype(BF16)

    def d_copy(n):
        return pltpu.make_async_remote_copy(
            d_send, d_buf.at[j], d_ss.at[n], d_rs.at[n], ((j + n) % DP, i), MESH
        )

    for n in (4, 3, 5, 2, 6, 1, 7):
        d_copy(n).start()
    d_buf[j] = d_send[...]
    for n in range(1, DP):
        d_copy(n).wait_recv()

    d_all = d_buf[...].astype(F32)
    rows = jnp.concatenate(
        [d_all[:, h * 8 : h * 8 + 8, :].reshape(DP * ROWS, HD).astype(BF16) for h in range(HEADS)], axis=1
    )
    none = jnp.zeros_like(rows)
    both = jnp.concatenate(
        [jnp.concatenate([rows, none], axis=1), jnp.concatenate([none, rows], axis=1)], axis=0
    )

    def o_copy(part, n, m):
        to = (x + n) % 4 * 4 + (y + m) % 4
        at = pl.ds(0, 1) if part == 0 else pl.ds(1, 3)
        return pltpu.make_async_remote_copy(
            o_send.at[to, at], o_buf.at[p, at], o_ss.at[part, n * 4 + m], o_rs.at[part, n * 4 + m], (j, z * NP + to), MESH
        )

    o_send[:, 0] = dot_nt(wt[0:256, :], both).astype(BF16).reshape(NP, 16, 128)
    for n, m in FAR:
        o_copy(0, n, m).start()
    for k in range(1, NZ):
        o_send[:, k] = dot_nt(wt[k * 256 : k * 256 + 256, :], both).astype(BF16).reshape(NP, 16, 128)
    for n, m in FAR:
        o_copy(1, n, m).start()

    def f_copy(k):
        to = (z + SLOTS[k]) % NZ
        return pltpu.make_async_remote_copy(
            f_send.at[k], f_buf.at[k], f_ss.at[k], f_rs.at[k], (j, to * NP + p), MESH
        )

    def source(n, m):
        return (x + 4 - n) % 4 * 4 + (y + 4 - m) % 4

    total = o_send[p, 0].astype(F32)
    for n, m in NEAR:
        o_copy(0, n, m).wait_recv()
        total = total + o_buf[source(n, m), 0].astype(F32)
    f_send[0] = total.astype(BF16)
    f_copy(0).start()
    totals = o_send[p, 1:4].astype(F32)
    for n, m in NEAR:
        o_copy(1, n, m).wait_recv()
        totals = totals + o_buf[source(n, m), 1:4].astype(F32)
    for k in (1, 2):
        f_send[k] = totals[k - 1].astype(BF16)
        f_copy(k).start()
    result = totals[2]
    for k in (1, 2, 0):
        f_copy(k).wait_recv()
        result = result + f_buf[k].astype(F32)
    result = jnp.concatenate([result[:, :64], result[:, 64:]], axis=0)
    out_ref[...] = (res_v[...].astype(F32) + result).astype(BF16)

    z_copy(0, z, facing).wait_send()
    z_copy(1, z, pair).wait_send()
    z_copy(2, z, across).wait_send()
    for n in range(1, DP):
        d_copy(n).wait_send()
    for n, m in FAR:
        p_copy(n, m).wait_send()
        o_copy(0, n, m).wait_send()
        o_copy(1, n, m).wait_send()
    for k in range(NZ - 1):
        f_copy(k).wait_send()


def local(
    queries, cache_keys, cache_values, new_keys, new_values, key_index, value_index, scale_table, lengths,
    head_mix, channel_mix, out_weight, residual,
):
    vmem, dma = pltpu.VMEM, pltpu.SemaphoreType.DMA
    turned = pl.pallas_call(
        kernel,
        out_shape=jax.ShapeDtypeStruct((32, 64), BF16),
        in_specs=[pl.BlockSpec(memory_space=pl.ANY)] * 13,
        out_specs=pl.BlockSpec(memory_space=pltpu.VMEM),
        scratch_shapes=[
            vmem((SEQ, STEPS, HEADS, HD), BF16),
            vmem((SEQ, CACHE, HD), BF16),
            vmem((SEQ, CACHE, HD), BF16),
            vmem((SEQ, STEPS, HD), BF16),
            vmem((SEQ, STEPS, HD), BF16),
            vmem((1, HD), jnp.int32),
            vmem((1, HD), jnp.int32),
            pltpu.SMEM((16,), F32),
            pltpu.SMEM((SEQ,), jnp.int32),
            vmem((128, 128), F32),
            vmem((128, 128), F32),
            vmem((256, 2048), BF16),
            vmem((32, 64), BF16),
            vmem((1024, 512), BF16),
            vmem((256, 128), BF16),
            vmem((NZ, 16, HD), BF16),
            vmem((NP, 16, HD), BF16),
            vmem((NP, 16, HD), BF16),
            vmem((16, HD), BF16),
            vmem((DP, 16, HD), BF16),
            vmem((NP, NZ, 16, 128), BF16),
            vmem((NP, NZ, 16, 128), BF16),
            vmem((NZ - 1, 16, 128), BF16),
            vmem((NZ - 1, 16, 128), BF16),
            dma((11,)),
            dma((SEQ,)),
            dma((SEQ,)),
            dma((NZ,)), dma((NZ,)),
            dma((NP,)), dma((NP,)),
            dma((DP,)), dma((DP,)),
            dma((2, NP)), dma((2, NP)),
            dma((NZ,)), dma((NZ,)),
        ],
        compiler_params=pltpu.CompilerParams(
            collective_id=0, has_side_effects=True, vmem_limit_bytes=60 * 1024 * 1024
        ),
    )(
        queries,
        cache_keys.reshape(SEQ, CACHE, HD),
        cache_values.reshape(SEQ, CACHE, HD),
        new_keys.reshape(SEQ, STEPS, HD),
        new_values.reshape(SEQ, STEPS, HD),
        key_index, value_index, scale_table, lengths, head_mix, channel_mix, out_weight, residual.T,
    )
    return turned.T


def solution(mesh):
    in_specs = (
        P("dp", None, "head", None),
        P("dp", None, "head", None),
        P("dp", None, "head", None),
        P("dp", None, "head", None),
        P("dp", None, "head", None),
        P("head", None),
        P("head", None),
        P(),
        P("dp"),
        P(),
        P(),
        P("head", "dp"),
        P(None, ("dp", "head")),
    )
    out_specs = P(None, ("dp", "head"))
    return jax.shard_map(local, mesh=mesh, in_specs=in_specs, out_specs=out_specs, check_vma=False)
```

```python
import functools

import jax
import jax.numpy as jnp
from jax import lax
from jax.experimental import pallas as pl
from jax.experimental.pallas import tpu as pltpu
from jax.sharding import PartitionSpec as P

MESH = pl.DeviceIdType.MESH
F32, BF16 = jnp.float32, jnp.bfloat16
DP, NZ, NP = 8, 4, 16
SEQ, STEPS, HEADS, HD, CACHE = 4, 2, 2, 128, 1024
ROWS = SEQ * STEPS
FAR = [(n, m) for n in (2, 1, 3, 0) for m in (2, 1, 3, 0) if n or m]
NEAR = sorted(FAR, key=lambda at: min(at[0], 4 - at[0]) + min(at[1], 4 - at[1]))
FAR_Z = (8, 7, 9, 6, 10, 5, 11, 4, 12, 3, 13, 2, 14, 1, 15)
SLOTS = (2, 1, 3, 0)
NT = (((1,), (1,)), ((), ()))


def split2(x):
    high = x.astype(BF16)
    return high, (x - high.astype(F32)).astype(BF16)


def dot(a, b):
    return jnp.dot(a, b, preferred_element_type=F32)


def dot_nt(a, b):
    return lax.dot_general(a, b, NT, preferred_element_type=F32)


def kernel(
    q_hbm, k_hbm, v_hbm, nk_hbm, nv_hbm, ki_hbm, vi_hbm, tab_hbm, len_hbm, hm_hbm, cm_hbm, w_hbm, res_hbm,
    out_ref,
    q_v, k_v, v_v, nk_v, nv_v, ki_v, vi_v, tab_s, len_s, hm_v, cm_v, w_v, res_v,
    wt, kron, a_buf, b_send, b_buf, d_buf, o_send, o_buf, f_send, f_buf,
    in_sem, k_sem, v_sem, far_sem,
    a_ss, a_rs, b_ss, b_rs, d_ss, d_rs, o_ss, o_rs, f_ss, f_rs,
):
    j = lax.axis_index("dp")
    i = lax.axis_index("head")
    c = j % 2
    z = i // NP
    zz = z * 4 + j // 2
    p = i % NP
    x = p // 4
    y = p % 4

    barrier = pltpu.get_barrier_semaphore()

    def hello(device):
        pl.semaphore_signal(barrier, inc=1, device_id=device, device_id_type=MESH)

    def along(n):
        to = (zz + n) % 16
        return to % 4 * 2 + c, to // 4 * NP + p

    def plane(n, m):
        return j, z * NP + (x + n) % 4 * 4 + (y + m) % 4

    sibling = (j + 1 - 2 * c, i)
    for n, m in FAR:
        hello(plane(n, m))
    for n in (4, 12, 3, 13, 2, 14, 1, 15):
        hello(along(n))
    hello(sibling)

    small = [
        (hm_hbm, hm_v), (cm_hbm, cm_v), (q_hbm, q_v), (ki_hbm, ki_v), (tab_hbm, tab_s), (len_hbm, len_s),
        (nk_hbm, nk_v), (nv_hbm, nv_v), (vi_hbm, vi_v), (res_hbm, res_v), (w_hbm, w_v),
    ]
    loads = [pltpu.make_async_copy(a, b, in_sem.at[n]) for n, (a, b) in enumerate(small)]
    k_loads = [pltpu.make_async_copy(k_hbm.at[s], k_v.at[s], k_sem.at[s]) for s in range(SEQ)]
    v_loads = [pltpu.make_async_copy(v_hbm.at[s], v_v.at[s], v_sem.at[s]) for s in range(SEQ)]
    for load in loads[:-1] + k_loads + v_loads:
        load.start()
    loads[-1].start()

    for load in loads[:2]:
        load.wait()

    m_row = lax.broadcasted_iota(jnp.int32, (NZ * 16, 128), 0)
    m_col = lax.broadcasted_iota(jnp.int32, (NZ * 16, 128), 1)
    pick_h = (m_col == m_row // 16 * 32 + p * 2 + m_row // 8 % 2).astype(F32)
    g_row = lax.broadcasted_iota(jnp.int32, (128, NP * 16), 0)
    g_col = lax.broadcasted_iota(jnp.int32, (128, NP * 16), 1)
    pick_g = (g_row == z * 32 + g_col // 8).astype(F32)
    wide = lax.dot_general(pick_h, hm_v[...], NT, precision=lax.Precision.HIGHEST, preferred_element_type=F32)
    wide = jnp.dot(wide, pick_g, precision=lax.Precision.HIGHEST, preferred_element_type=F32)
    a_row = lax.broadcasted_iota(jnp.int32, (NZ * 16, NP * 16), 0)
    a_col = lax.broadcasted_iota(jnp.int32, (NZ * 16, NP * 16), 1)
    wide = jnp.where(a_row % 8 == a_col % 8, wide, 0.0)
    wide_h, wide_l = split2(wide)
    kron[...] = jnp.concatenate([wide_h, wide_l], axis=1)
    c_h, c_l = split2(cm_v[...])
    chan = jnp.concatenate([c_h, c_l, c_h], axis=0)

    for load in loads[2:-1]:
        load.wait()
    key_scale = jnp.zeros((1, HD), F32)
    value_scale = jnp.zeros((1, HD), F32)
    for n in range(16):
        key_scale = jnp.where(ki_v[...] == n, tab_s[n], key_scale)
        value_scale = jnp.where(vi_v[...] == n, tab_s[n], value_scale)
    q_all = q_v[...].astype(F32)
    q = jnp.concatenate(
        [q_all[s, t, h : h + 1, :] for h in range(HEADS) for s in range(SEQ) for t in range(STEPS)], axis=0
    )
    scaled = (q * key_scale).astype(BF16)
    q_b = q.astype(BF16)
    nk_all = nk_v[...].astype(F32)
    nv_all = nv_v[...].astype(F32)
    nk = jnp.concatenate([nk_all[s] for s in range(SEQ)], axis=0).astype(BF16)
    nv = jnp.concatenate([nv_all[s] for s in range(SEQ)], axis=0).astype(BF16)

    row = lax.broadcasted_iota(jnp.int32, (16, CACHE), 0)
    row_seq = row % 8 // 2
    score = jnp.zeros((16, CACHE), F32)
    length = jnp.zeros((16, CACHE), jnp.int32)
    for s in range(SEQ):
        k_loads[s].wait()
        score = jnp.where(row_seq == s, dot_nt(scaled, k_v[s]), score)
        length = jnp.where(row_seq == s, len_s[s], length)
    inverse = 1.0 / HD**0.5
    place = lax.broadcasted_iota(jnp.int32, (16, CACHE), 1)
    score = jnp.where(place < length, score * inverse, -jnp.inf)
    new_row = lax.broadcasted_iota(jnp.int32, (16, 8), 0)
    new_col = lax.broadcasted_iota(jnp.int32, (16, 8), 1)
    seen = (new_row % 8 // 2 == new_col // 2) & (new_col % 2 <= new_row % 2)
    new_score = jnp.where(seen, dot_nt(q_b, nk) * inverse, -jnp.inf)
    top = jnp.maximum(jnp.max(score, axis=1, keepdims=True), jnp.max(new_score, axis=1, keepdims=True))
    weight = jnp.exp(score - top)
    new_weight = jnp.exp(new_score - top)
    total = jnp.sum(weight, axis=1, keepdims=True) + jnp.sum(new_weight, axis=1, keepdims=True)
    weight = weight.astype(BF16)
    attended = jnp.zeros((16, HD), F32)
    for s in range(SEQ):
        v_loads[s].wait()
        attended = jnp.where(row_seq[:, :HD] == s, dot(weight, v_v[s]), attended)
    attended = (attended * value_scale + dot(new_weight.astype(BF16), nv)) / total
    a_h, a_l = split2(attended)
    inner = dot(jnp.concatenate([a_h, a_h, a_l], axis=1), chan)
    a_buf[p] = inner.astype(BF16)

    pl.semaphore_wait(barrier, NP - 1 + 8 + 1)
    for n in (4, 12):
        pl.semaphore_signal(far_sem, inc=1, device_id=along(n), device_id_type=MESH)

    def a_copy(n, m):
        return pltpu.make_async_remote_copy(
            a_buf.at[p], a_buf.at[p], a_ss.at[n * 4 + m], a_rs.at[n * 4 + m], plane(n, m), MESH
        )

    for n, m in FAR:
        a_copy(n, m).start()

    loads[-1].wait()
    for k, n in enumerate(SLOTS):
        first = (z + n) % NZ * 512

        @pl.loop(0, 4)
        def _(t, k=k, first=first):
            turned = w_v[:, pl.ds(pl.multiple_of(first + t * 128, 128), 128)].astype(F32).T.astype(BF16)
            for n in range(8):
                start = pl.multiple_of(k * 256 + (t * 4 + n // 2) * 16, 16)
                wt[pl.ds(start, 16), n % 2 * 256 : n % 2 * 256 + 256] = turned[n * 16 : n * 16 + 16, :]

    for n, m in NEAR:
        a_copy(n, m).wait_recv()

    held = a_buf[...].reshape(NP * 16, HD)
    b_send[...] = dot(kron[...], jnp.concatenate([held, held], axis=0)).astype(BF16).reshape(NZ, 16, HD)
    pl.semaphore_wait(far_sem, 2)

    def b_copy(n):
        to = (zz + n) % 16
        return pltpu.make_async_remote_copy(
            b_send.at[to // 4], b_buf.at[zz], b_ss.at[n], b_rs.at[n], along(n), MESH
        )

    for n in FAR_Z:
        b_copy(n).start()
    b_buf[zz] = b_send[z]
    for n in reversed(FAR_Z):
        b_copy(n).wait_recv()
    mixed = b_buf[0:4].astype(F32)
    for n in range(1, NZ):
        mixed = mixed + b_buf[n * 4 : n * 4 + 4].astype(F32)

    d_buf[c] = mixed.astype(BF16)
    swap = pltpu.make_async_remote_copy(d_buf.at[c], d_buf.at[c], d_ss.at[0], d_rs.at[0], sibling, MESH)
    swap.start()
    swap.wait_recv()

    d_all = d_buf[...].astype(F32)
    rows = jnp.concatenate(
        [
            jnp.concatenate([d_all[n % 2, n // 2, h * 8 : h * 8 + 8, :] for n in range(DP)], axis=0).astype(BF16)
            for h in range(HEADS)
        ],
        axis=1,
    )
    none = jnp.zeros_like(rows)
    both = jnp.concatenate(
        [jnp.concatenate([rows, none], axis=1), jnp.concatenate([none, rows], axis=1)], axis=0
    )

    def o_copy(part, n, m):
        to = (x + n) % 4 * 4 + (y + m) % 4
        at = pl.ds(0, 1) if part == 0 else pl.ds(1, 3)
        return pltpu.make_async_remote_copy(
            o_send.at[to, at], o_buf.at[p, at], o_ss.at[part, n * 4 + m], o_rs.at[part, n * 4 + m], (j, z * NP + to), MESH
        )

    o_send[:, 0] = dot_nt(wt[0:256, :], both).astype(BF16).reshape(NP, 16, 128)
    for n, m in FAR:
        o_copy(0, n, m).start()
    for k in range(1, NZ):
        o_send[:, k] = dot_nt(wt[k * 256 : k * 256 + 256, :], both).astype(BF16).reshape(NP, 16, 128)
    for n, m in FAR:
        o_copy(1, n, m).start()

    def f_copy(k):
        to = (z + SLOTS[k]) % NZ
        return pltpu.make_async_remote_copy(
            f_send.at[k], f_buf.at[k], f_ss.at[k], f_rs.at[k], (j, to * NP + p), MESH
        )

    def source(n, m):
        return (x + 4 - n) % 4 * 4 + (y + 4 - m) % 4

    total = o_send[p, 0].astype(F32)
    for n, m in NEAR:
        o_copy(0, n, m).wait_recv()
        total = total + o_buf[source(n, m), 0].astype(F32)
    f_send[0] = total.astype(BF16)
    f_copy(0).start()
    totals = o_send[p, 1:4].astype(F32)
    for n, m in NEAR:
        o_copy(1, n, m).wait_recv()
        totals = totals + o_buf[source(n, m), 1:4].astype(F32)
    for k in (1, 2):
        f_send[k] = totals[k - 1].astype(BF16)
        f_copy(k).start()
    result = totals[2]
    for k in (1, 2, 0):
        f_copy(k).wait_recv()
        result = result + f_buf[k].astype(F32)
    result = jnp.concatenate([result[:, :64], result[:, 64:]], axis=0)
    out_ref[...] = (res_v[...].astype(F32) + result).astype(BF16)

    for n, m in FAR:
        a_copy(n, m).wait_send()
        o_copy(0, n, m).wait_send()
        o_copy(1, n, m).wait_send()
    for n in FAR_Z:
        b_copy(n).wait_send()
    swap.wait_send()
    for k in range(NZ - 1):
        f_copy(k).wait_send()


def local(
    queries, cache_keys, cache_values, new_keys, new_values, key_index, value_index, scale_table, lengths,
    head_mix, channel_mix, out_weight, residual,
):
    vmem, dma = pltpu.VMEM, pltpu.SemaphoreType.DMA
    turned = pl.pallas_call(
        kernel,
        out_shape=pltpu.VMEM((32, 64), BF16),
        in_specs=[pl.BlockSpec(memory_space=pl.ANY)] * 13,
        out_specs=pl.BlockSpec(memory_space=pltpu.VMEM),
        scratch_shapes=[
            vmem((SEQ, STEPS, HEADS, HD), BF16),
            vmem((SEQ, CACHE, HD), BF16),
            vmem((SEQ, CACHE, HD), BF16),
            vmem((SEQ, STEPS, HD), BF16),
            vmem((SEQ, STEPS, HD), BF16),
            vmem((1, HD), jnp.int32),
            vmem((1, HD), jnp.int32),
            pltpu.SMEM((16,), F32),
            pltpu.SMEM((SEQ,), jnp.int32),
            vmem((128, 128), F32),
            vmem((128, 128), F32),
            vmem((256, 2048), BF16),
            vmem((32, 64), BF16),
            vmem((1024, 512), BF16),
            vmem((64, 512), BF16),
            vmem((NP, 16, HD), BF16),
            vmem((NZ, 16, HD), BF16),
            vmem((16, 16, HD), BF16),
            vmem((2, NZ, 16, HD), BF16),
            vmem((NP, NZ, 16, 128), BF16),
            vmem((NP, NZ, 16, 128), BF16),
            vmem((NZ - 1, 16, 128), BF16),
            vmem((NZ - 1, 16, 128), BF16),
            dma((11,)),
            dma((SEQ,)),
            dma((SEQ,)),
            pltpu.SemaphoreType.REGULAR,
            dma((NP,)), dma((NP,)),
            dma((16,)), dma((16,)),
            dma((1,)), dma((1,)),
            dma((2, NP)), dma((2, NP)),
            dma((NZ,)), dma((NZ,)),
        ],
        compiler_params=pltpu.CompilerParams(
            collective_id=0, has_side_effects=True, vmem_limit_bytes=60 * 1024 * 1024
        ),
    )(
        queries,
        cache_keys.reshape(SEQ, CACHE, HD),
        cache_values.reshape(SEQ, CACHE, HD),
        new_keys.reshape(SEQ, STEPS, HD),
        new_values.reshape(SEQ, STEPS, HD),
        key_index, value_index, scale_table, lengths, head_mix, channel_mix, out_weight, residual.T,
    )
    return turned.T


def solution(mesh):
    in_specs = (
        P("dp", None, "head", None),
        P("dp", None, "head", None),
        P("dp", None, "head", None),
        P("dp", None, "head", None),
        P("dp", None, "head", None),
        P("head", None),
        P("head", None),
        P(),
        P("dp"),
        P(),
        P(),
        P("head", "dp"),
        P(None, ("dp", "head")),
    )
    out_specs = P(None, ("dp", "head"))
    return jax.shard_map(local, mesh=mesh, in_specs=in_specs, out_specs=out_specs, check_vma=False)
```

```python
import functools

import jax
import jax.numpy as jnp
from jax import lax
from jax.experimental import pallas as pl
from jax.experimental.pallas import tpu as pltpu
from jax.sharding import PartitionSpec as P

MESH = pl.DeviceIdType.MESH
F32, BF16 = jnp.float32, jnp.bfloat16
DP, NZ, NP = 8, 4, 16
SEQ, STEPS, HEADS, HD, CACHE = 4, 2, 2, 128, 1024
ROWS = SEQ * STEPS
FAR = [(n, m) for n in (2, 1, 3, 0) for m in (2, 1, 3, 0) if n or m]
NEAR = sorted(FAR, key=lambda at: min(at[0], 4 - at[0]) + min(at[1], 4 - at[1]))
FAR_Z = (8, 7, 9, 6, 10, 5, 11, 4, 12, 3, 13, 2, 14, 1, 15)
NT = (((1,), (1,)), ((), ()))


def split2(x):
    high = x.astype(BF16)
    return high, (x - high.astype(F32)).astype(BF16)


def dot(a, b):
    return jnp.dot(a, b, preferred_element_type=F32)


def dot_nt(a, b):
    return lax.dot_general(a, b, NT, preferred_element_type=F32)


def kernel(
    q_hbm, k_hbm, v_hbm, nk_hbm, nv_hbm, ki_hbm, vi_hbm, tab_hbm, len_hbm, hm_hbm, cm_hbm, w_hbm, res_hbm,
    out_ref,
    q_v, k_v, v_v, nk_v, nv_v, ki_v, vi_v, tab_s, len_s, hm_v, cm_v, w_v, res_v,
    wt, kron, a_buf, b_send, b_buf, d_buf, o_send, o_buf, e_buf, t_buf, f_send, f_buf,
    in_sem, k_sem, v_sem, far_sem,
    a_ss, a_rs, b_ss, b_rs, d_ss, d_rs, o_ss, o_rs, e_ss, e_rs, f_ss, f_rs,
):
    j = lax.axis_index("dp")
    i = lax.axis_index("head")
    c = j % 2
    z = i // NP
    zz = z * 4 + j // 2
    p = i % NP
    x = p // 4
    y = p % 4

    barrier = pltpu.get_barrier_semaphore()

    def hello(device):
        pl.semaphore_signal(barrier, inc=1, device_id=device, device_id_type=MESH)

    def along(n):
        to = (zz + n) % 16
        return to % 4 * 2 + c, to // 4 * NP + p

    def plane(n, m):
        return j, z * NP + (x + n) % 4 * 4 + (y + m) % 4

    sibling = (j + 1 - 2 * c, i)
    for n, m in FAR:
        hello(plane(n, m))
    for n in (4, 12, 3, 13, 2, 14, 1, 15):
        hello(along(n))
    hello(sibling)

    small = [
        (hm_hbm, hm_v), (cm_hbm, cm_v), (q_hbm, q_v), (ki_hbm, ki_v), (tab_hbm, tab_s), (len_hbm, len_s),
        (nk_hbm, nk_v), (nv_hbm, nv_v), (vi_hbm, vi_v), (res_hbm, res_v), (w_hbm, w_v),
    ]
    loads = [pltpu.make_async_copy(a, b, in_sem.at[n]) for n, (a, b) in enumerate(small)]
    k_loads = [pltpu.make_async_copy(k_hbm.at[s], k_v.at[s], k_sem.at[s]) for s in range(SEQ)]
    v_loads = [pltpu.make_async_copy(v_hbm.at[s], v_v.at[s], v_sem.at[s]) for s in range(SEQ)]
    for load in loads[:-1] + k_loads + v_loads:
        load.start()
    loads[-1].start()

    for load in loads[:2]:
        load.wait()

    m_row = lax.broadcasted_iota(jnp.int32, (NZ * 16, 128), 0)
    m_col = lax.broadcasted_iota(jnp.int32, (NZ * 16, 128), 1)
    pick_h = (m_col == m_row // 16 * 32 + p * 2 + m_row // 8 % 2).astype(F32)
    g_row = lax.broadcasted_iota(jnp.int32, (128, NP * 16), 0)
    g_col = lax.broadcasted_iota(jnp.int32, (128, NP * 16), 1)
    pick_g = (g_row == z * 32 + g_col // 8).astype(F32)
    wide = lax.dot_general(pick_h, hm_v[...], NT, precision=lax.Precision.HIGHEST, preferred_element_type=F32)
    wide = jnp.dot(wide, pick_g, precision=lax.Precision.HIGHEST, preferred_element_type=F32)
    a_row = lax.broadcasted_iota(jnp.int32, (NZ * 16, NP * 16), 0)
    a_col = lax.broadcasted_iota(jnp.int32, (NZ * 16, NP * 16), 1)
    wide = jnp.where(a_row % 8 == a_col % 8, wide, 0.0)
    wide_h, wide_l = split2(wide)
    kron[...] = jnp.concatenate([wide_h, wide_l], axis=1)
    c_h, c_l = split2(cm_v[...])
    chan = jnp.concatenate([c_h, c_l, c_h], axis=0)

    for load in loads[2:-1]:
        load.wait()
    key_scale = jnp.zeros((1, HD), F32)
    value_scale = jnp.zeros((1, HD), F32)
    for n in range(16):
        key_scale = jnp.where(ki_v[...] == n, tab_s[n], key_scale)
        value_scale = jnp.where(vi_v[...] == n, tab_s[n], value_scale)
    q_all = q_v[...].astype(F32)
    q = jnp.concatenate(
        [q_all[s, t, h : h + 1, :] for h in range(HEADS) for s in range(SEQ) for t in range(STEPS)], axis=0
    )
    scaled = (q * key_scale).astype(BF16)
    q_b = q.astype(BF16)
    nk_all = nk_v[...].astype(F32)
    nv_all = nv_v[...].astype(F32)
    nk = jnp.concatenate([nk_all[s] for s in range(SEQ)], axis=0).astype(BF16)
    nv = jnp.concatenate([nv_all[s] for s in range(SEQ)], axis=0).astype(BF16)

    row = lax.broadcasted_iota(jnp.int32, (16, CACHE), 0)
    row_seq = row % 8 // 2
    score = jnp.zeros((16, CACHE), F32)
    length = jnp.zeros((16, CACHE), jnp.int32)
    for s in range(SEQ):
        k_loads[s].wait()
        score = jnp.where(row_seq == s, dot_nt(scaled, k_v[s]), score)
        length = jnp.where(row_seq == s, len_s[s], length)
    inverse = 1.0 / HD**0.5
    place = lax.broadcasted_iota(jnp.int32, (16, CACHE), 1)
    score = jnp.where(place < length, score * inverse, -jnp.inf)
    new_row = lax.broadcasted_iota(jnp.int32, (16, 8), 0)
    new_col = lax.broadcasted_iota(jnp.int32, (16, 8), 1)
    seen = (new_row % 8 // 2 == new_col // 2) & (new_col % 2 <= new_row % 2)
    new_score = jnp.where(seen, dot_nt(q_b, nk) * inverse, -jnp.inf)
    top = jnp.maximum(jnp.max(score, axis=1, keepdims=True), jnp.max(new_score, axis=1, keepdims=True))
    weight = jnp.exp(score - top)
    new_weight = jnp.exp(new_score - top)
    total = jnp.sum(weight, axis=1, keepdims=True) + jnp.sum(new_weight, axis=1, keepdims=True)
    weight = weight.astype(BF16)
    attended = jnp.zeros((16, HD), F32)
    for s in range(SEQ):
        v_loads[s].wait()
        attended = jnp.where(row_seq[:, :HD] == s, dot(weight, v_v[s]), attended)
    attended = (attended * value_scale + dot(new_weight.astype(BF16), nv)) / total
    a_h, a_l = split2(attended)
    inner = dot(jnp.concatenate([a_h, a_h, a_l], axis=1), chan)
    a_buf[p] = inner.astype(BF16)

    pl.semaphore_wait(barrier, NP - 1 + 8 + 1)
    for n in (4, 12):
        pl.semaphore_signal(far_sem, inc=1, device_id=along(n), device_id_type=MESH)

    def a_copy(n, m):
        return pltpu.make_async_remote_copy(
            a_buf.at[p], a_buf.at[p], a_ss.at[n * 4 + m], a_rs.at[n * 4 + m], plane(n, m), MESH
        )

    for n, m in FAR:
        a_copy(n, m).start()

    loads[-1].wait()

    @pl.loop(0, 16)
    def _(t):
        turned = w_v[:, pl.ds(pl.multiple_of(t * 128, 128), 128)].astype(F32).T.astype(BF16)
        for n in range(8):
            start = pl.multiple_of(t // 4 * 256 + (t % 4 * 4 + n // 2) * 16, 16)
            wt[pl.ds(start, 16), n % 2 * 256 : n % 2 * 256 + 256] = turned[n * 16 : n * 16 + 16, :]

    for n, m in NEAR:
        a_copy(n, m).wait_recv()

    held = a_buf[...].reshape(NP * 16, HD)
    b_send[...] = dot(kron[...], jnp.concatenate([held, held], axis=0)).astype(BF16).reshape(NZ, 16, HD)
    pl.semaphore_wait(far_sem, 2)

    def b_copy(n):
        to = (zz + n) % 16
        return pltpu.make_async_remote_copy(
            b_send.at[to // 4], b_buf.at[zz], b_ss.at[n], b_rs.at[n], along(n), MESH
        )

    for n in FAR_Z:
        b_copy(n).start()
    b_buf[zz] = b_send[z]
    for n in reversed(FAR_Z):
        b_copy(n).wait_recv()
    mixed = b_buf[0:4].astype(F32)
    for n in range(1, NZ):
        mixed = mixed + b_buf[n * 4 : n * 4 + 4].astype(F32)

    d_buf[c] = mixed.astype(BF16)
    swap = pltpu.make_async_remote_copy(d_buf.at[c], d_buf.at[c], d_ss.at[0], d_rs.at[0], sibling, MESH)
    swap.start()
    swap.wait_recv()

    d_all = d_buf[...].astype(F32)
    rows = jnp.concatenate(
        [
            jnp.concatenate([d_all[n % 2, n // 2, h * 8 : h * 8 + 8, :] for n in range(DP)], axis=0).astype(BF16)
            for h in range(HEADS)
        ],
        axis=1,
    )
    none = jnp.zeros_like(rows)
    both = jnp.concatenate(
        [jnp.concatenate([rows, none], axis=1), jnp.concatenate([none, rows], axis=1)], axis=0
    )

    def o_copy(part, n, m):
        to = (x + n) % 4 * 4 + (y + m) % 4
        at = pl.ds(0, 1) if part == 0 else pl.ds(1, 3)
        return pltpu.make_async_remote_copy(
            o_send.at[to, at], o_buf.at[p, at], o_ss.at[part, n * 4 + m], o_rs.at[part, n * 4 + m], (j, z * NP + to), MESH
        )

    def e_copy(n, m):
        to = (x + n) % 4 * 4 + (y + m) % 4
        return pltpu.make_async_remote_copy(
            o_send.at[to, 0], e_buf.at[p], e_ss.at[n * 4 + m], e_rs.at[n * 4 + m], (j, to), MESH
        )

    straight = zz == 8
    o_send[:, 0] = dot_nt(wt[0:256, :], both).astype(BF16).reshape(NP, 16, 128)

    @pl.when(straight)
    def _():
        for n, m in FAR + [(0, 0)]:
            e_copy(n, m).start()

    @pl.when(jnp.logical_not(straight))
    def _():
        for n, m in FAR:
            o_copy(0, n, m).start()

    for k in range(1, NZ):
        o_send[:, k] = dot_nt(wt[k * 256 : k * 256 + 256, :], both).astype(BF16).reshape(NP, 16, 128)
    for n, m in FAR:
        o_copy(1, n, m).start()

    def f_copy(to):
        return pltpu.make_async_remote_copy(
            f_send.at[to], f_buf.at[z], f_ss.at[to], f_rs.at[z], (j, to * NP + p), MESH
        )

    def f_wait(origin):
        pltpu.make_async_remote_copy(
            f_send.at[0], f_buf.at[origin], f_ss.at[0], f_rs.at[origin], (j, (z + 1) % NZ * NP + p), MESH
        ).wait_recv()

    def source(n, m):
        return (x + 4 - n) % 4 * 4 + (y + 4 - m) % 4

    @pl.when(jnp.logical_not(straight))
    def _():
        total = o_send[p, 0].astype(F32)
        for n, m in NEAR:
            o_copy(0, n, m).wait_recv()
            total = total + o_buf[source(n, m), 0].astype(F32)
        t_buf[0] = total
        f_send[0] = total.astype(BF16)

        @pl.when(z > 0)
        def _():
            f_copy(0).start()

    totals = o_send[p, 1:4].astype(F32)
    for n, m in NEAR:
        o_copy(1, n, m).wait_recv()
        totals = totals + o_buf[source(n, m), 1:4].astype(F32)
    t_buf[1:4] = totals
    f_send[1:4] = totals.astype(BF16)
    for n in (2, 1, 3):
        to = (z + n) % NZ

        @pl.when(to > 0)
        def _(to=to):
            f_copy(to).start()

    t_buf[NZ] = t_buf[z]
    for n in (1, 3):
        f_wait((z + n) % NZ)
        t_buf[NZ] += f_buf[(z + n) % NZ].astype(F32)

    @pl.when(zz == 0)
    def _():
        extra = jnp.zeros((16, 128), F32)
        for n, m in [(0, 0)] + NEAR:
            e_copy(n, m).wait_recv()
            extra = extra + e_buf[source(n, m)].astype(F32)
        t_buf[NZ] += extra

    @pl.when(zz != 0)
    def _():
        f_wait((z + 2) % NZ)
        t_buf[NZ] += f_buf[(z + 2) % NZ].astype(F32)

    result = t_buf[NZ]
    result = jnp.concatenate([result[:, :64], result[:, 64:]], axis=0)
    out_ref[...] = (res_v[...].astype(F32) + result).astype(BF16)

    for n, m in FAR:
        a_copy(n, m).wait_send()
        o_copy(1, n, m).wait_send()

    @pl.when(straight)
    def _():
        for n, m in FAR + [(0, 0)]:
            e_copy(n, m).wait_send()

    @pl.when(jnp.logical_not(straight))
    def _():
        for n, m in FAR:
            o_copy(0, n, m).wait_send()

    for n in FAR_Z:
        b_copy(n).wait_send()
    swap.wait_send()
    for to in range(NZ):
        moved = jnp.logical_and(z != to, jnp.logical_not(straight)) if to == 0 else z != to

        @pl.when(moved)
        def _(to=to):
            f_copy(to).wait_send()


def local(
    queries, cache_keys, cache_values, new_keys, new_values, key_index, value_index, scale_table, lengths,
    head_mix, channel_mix, out_weight, residual,
):
    vmem, dma = pltpu.VMEM, pltpu.SemaphoreType.DMA
    turned = pl.pallas_call(
        kernel,
        out_shape=pltpu.VMEM((32, 64), BF16),
        in_specs=[pl.BlockSpec(memory_space=pl.ANY)] * 13,
        out_specs=pl.BlockSpec(memory_space=pltpu.VMEM),
        scratch_shapes=[
            vmem((SEQ, STEPS, HEADS, HD), BF16),
            vmem((SEQ, CACHE, HD), BF16),
            vmem((SEQ, CACHE, HD), BF16),
            vmem((SEQ, STEPS, HD), BF16),
            vmem((SEQ, STEPS, HD), BF16),
            vmem((1, HD), jnp.int32),
            vmem((1, HD), jnp.int32),
            pltpu.SMEM((16,), F32),
            pltpu.SMEM((SEQ,), jnp.int32),
            vmem((128, 128), F32),
            vmem((128, 128), F32),
            vmem((256, 2048), BF16),
            vmem((32, 64), BF16),
            vmem((1024, 512), BF16),
            vmem((64, 512), BF16),
            vmem((NP, 16, HD), BF16),
            vmem((NZ, 16, HD), BF16),
            vmem((16, 16, HD), BF16),
            vmem((2, NZ, 16, HD), BF16),
            vmem((NP, NZ, 16, 128), BF16),
            vmem((NP, NZ, 16, 128), BF16),
            vmem((NP, 16, 128), BF16),
            vmem((NZ + 1, 16, 128), F32),
            vmem((NZ, 16, 128), BF16),
            vmem((NZ, 16, 128), BF16),
            dma((11,)),
            dma((SEQ,)),
            dma((SEQ,)),
            pltpu.SemaphoreType.REGULAR,
            dma((NP,)), dma((NP,)),
            dma((16,)), dma((16,)),
            dma((1,)), dma((1,)),
            dma((2, NP)), dma((2, NP)),
            dma((NP,)), dma((NP,)),
            dma((NZ,)), dma((NZ,)),
        ],
        compiler_params=pltpu.CompilerParams(
            collective_id=0, has_side_effects=True, vmem_limit_bytes=60 * 1024 * 1024
        ),
    )(
        queries,
        cache_keys.reshape(SEQ, CACHE, HD),
        cache_values.reshape(SEQ, CACHE, HD),
        new_keys.reshape(SEQ, STEPS, HD),
        new_values.reshape(SEQ, STEPS, HD),
        key_index, value_index, scale_table, lengths, head_mix, channel_mix, out_weight, residual.T,
    )
    return turned.T


def solution(mesh):
    in_specs = (
        P("dp", None, "head", None),
        P("dp", None, "head", None),
        P("dp", None, "head", None),
        P("dp", None, "head", None),
        P("dp", None, "head", None),
        P("head", None),
        P("head", None),
        P(),
        P("dp"),
        P(),
        P(),
        P("head", "dp"),
        P(None, ("dp", "head")),
    )
    out_specs = P(None, ("dp", "head"))
    return jax.shard_map(local, mesh=mesh, in_specs=in_specs, out_specs=out_specs, check_vma=False)
```

```python
import functools

import jax
import jax.numpy as jnp
from jax import lax
from jax.experimental import pallas as pl
from jax.experimental.pallas import tpu as pltpu
from jax.sharding import PartitionSpec as P

MESH = pl.DeviceIdType.MESH
F32, BF16 = jnp.float32, jnp.bfloat16
DP, NZ, NP = 8, 4, 16
SEQ, STEPS, HEADS, HD, CACHE = 4, 2, 2, 128, 1024
ROWS = SEQ * STEPS
FAR = [(n, m) for n in (2, 1, 3, 0) for m in (2, 1, 3, 0) if n or m]
NEAR = sorted(FAR, key=lambda at: min(at[0], 4 - at[0]) + min(at[1], 4 - at[1]))
FIRST = (0, 1, 2, 3, 4, 8, 12, 5, 6, 7, 9, 10, 11, 13, 14, 15)
FAR_Z = (8, 7, 9, 6, 10, 5, 11, 4, 12, 3, 13, 2, 14, 1, 15)
NT = (((1,), (1,)), ((), ()))


def split2(x):
    high = x.astype(BF16)
    return high, (x - high.astype(F32)).astype(BF16)


def dot(a, b):
    return jnp.dot(a, b, preferred_element_type=F32)


def dot_nt(a, b):
    return lax.dot_general(a, b, NT, preferred_element_type=F32)


def kernel(
    q_hbm, k_hbm, v_hbm, nk_hbm, nv_hbm, ki_hbm, vi_hbm, tab_hbm, len_hbm, hm_hbm, cm_hbm, w_hbm, res_hbm,
    out_ref,
    q_v, k_v, v_v, nk_v, nv_v, ki_v, vi_v, tab_s, len_s, hm_v, cm_v, w_v, res_v,
    wt, kron, a_buf, b_send, b_buf, m_buf, o_send, o_buf, e_buf, t_buf, f_send, f_buf,
    in_sem, k_sem, v_sem, far_sem,
    a_ss, a_rs, b_ss, b_rs, d_ss, d_rs, o_ss, o_rs, e_ss, e_rs, f_ss, f_rs,
):
    j = lax.axis_index("dp")
    i = lax.axis_index("head")
    c = j % 2
    z = i // NP
    zz = z * 4 + j // 2
    p = i % NP
    x = p // 4
    y = p % 4

    barrier = pltpu.get_barrier_semaphore()

    def hello(device):
        pl.semaphore_signal(barrier, inc=1, device_id=device, device_id_type=MESH)

    def along(n):
        to = (zz + n) % 16
        return to % 4 * 2 + c, to // 4 * NP + p

    def plane(n, m):
        return j, z * NP + (x + n) % 4 * 4 + (y + m) % 4

    sibling = (j + 1 - 2 * c, i)
    for n, m in FAR:
        hello(plane(n, m))
    for n in (4, 12, 3, 13, 2, 14, 1, 15):
        hello(along(n))
    hello(sibling)

    small = [
        (hm_hbm, hm_v), (cm_hbm, cm_v), (q_hbm, q_v), (ki_hbm, ki_v), (tab_hbm, tab_s), (len_hbm, len_s),
        (nk_hbm, nk_v), (nv_hbm, nv_v), (vi_hbm, vi_v), (res_hbm, res_v), (w_hbm, w_v),
    ]
    loads = [pltpu.make_async_copy(a, b, in_sem.at[n]) for n, (a, b) in enumerate(small)]
    k_loads = [pltpu.make_async_copy(k_hbm.at[s], k_v.at[s], k_sem.at[s]) for s in range(SEQ)]
    v_loads = [pltpu.make_async_copy(v_hbm.at[s], v_v.at[s], v_sem.at[s]) for s in range(SEQ)]
    for load in loads[:-1] + k_loads + v_loads:
        load.start()
    loads[-1].start()

    for load in loads[:2]:
        load.wait()

    m_row = lax.broadcasted_iota(jnp.int32, (NZ * 16, 128), 0)
    m_col = lax.broadcasted_iota(jnp.int32, (NZ * 16, 128), 1)
    pick_h = (m_col == m_row // 16 * 32 + p * 2 + m_row // 8 % 2).astype(F32)
    g_row = lax.broadcasted_iota(jnp.int32, (128, NP * 16), 0)
    g_col = lax.broadcasted_iota(jnp.int32, (128, NP * 16), 1)
    pick_g = (g_row == z * 32 + g_col // 8).astype(F32)
    wide = lax.dot_general(pick_h, hm_v[...], NT, precision=lax.Precision.HIGHEST, preferred_element_type=F32)
    wide = jnp.dot(wide, pick_g, precision=lax.Precision.HIGHEST, preferred_element_type=F32)
    a_row = lax.broadcasted_iota(jnp.int32, (NZ * 16, NP * 16), 0)
    a_col = lax.broadcasted_iota(jnp.int32, (NZ * 16, NP * 16), 1)
    wide = jnp.where(a_row % 8 == a_col % 8, wide, 0.0)
    wide_h, wide_l = split2(wide)
    kron[...] = jnp.concatenate([wide_h, wide_l], axis=1)
    c_h, c_l = split2(cm_v[...])
    chan = jnp.concatenate([c_h, c_l, c_h], axis=0)

    for load in loads[2:-1]:
        load.wait()
    key_scale = jnp.zeros((1, HD), F32)
    value_scale = jnp.zeros((1, HD), F32)
    for n in range(16):
        key_scale = jnp.where(ki_v[...] == n, tab_s[n], key_scale)
        value_scale = jnp.where(vi_v[...] == n, tab_s[n], value_scale)
    q_all = q_v[...].astype(F32)
    q = jnp.concatenate(
        [q_all[s, t, h : h + 1, :] for h in range(HEADS) for s in range(SEQ) for t in range(STEPS)], axis=0
    )
    scaled = (q * key_scale).astype(BF16)
    q_b = q.astype(BF16)
    nk_all = nk_v[...].astype(F32)
    nv_all = nv_v[...].astype(F32)
    nk = jnp.concatenate([nk_all[s] for s in range(SEQ)], axis=0).astype(BF16)
    nv = jnp.concatenate([nv_all[s] for s in range(SEQ)], axis=0).astype(BF16)

    row = lax.broadcasted_iota(jnp.int32, (16, CACHE), 0)
    row_seq = row % 8 // 2
    score = jnp.zeros((16, CACHE), F32)
    length = jnp.zeros((16, CACHE), jnp.int32)
    for s in range(SEQ):
        k_loads[s].wait()
        score = jnp.where(row_seq == s, dot_nt(scaled, k_v[s]), score)
        length = jnp.where(row_seq == s, len_s[s], length)
    inverse = 1.0 / HD**0.5
    place = lax.broadcasted_iota(jnp.int32, (16, CACHE), 1)
    score = jnp.where(place < length, score * inverse, -jnp.inf)
    new_row = lax.broadcasted_iota(jnp.int32, (16, 8), 0)
    new_col = lax.broadcasted_iota(jnp.int32, (16, 8), 1)
    seen = (new_row % 8 // 2 == new_col // 2) & (new_col % 2 <= new_row % 2)
    new_score = jnp.where(seen, dot_nt(q_b, nk) * inverse, -jnp.inf)
    top = jnp.maximum(jnp.max(score, axis=1, keepdims=True), jnp.max(new_score, axis=1, keepdims=True))
    weight = jnp.exp(score - top)
    new_weight = jnp.exp(new_score - top)
    total = jnp.sum(weight, axis=1, keepdims=True) + jnp.sum(new_weight, axis=1, keepdims=True)
    weight = weight.astype(BF16)
    attended = jnp.zeros((16, HD), F32)
    for s in range(SEQ):
        v_loads[s].wait()
        attended = jnp.where(row_seq[:, :HD] == s, dot(weight, v_v[s]), attended)
    attended = (attended * value_scale + dot(new_weight.astype(BF16), nv)) / total
    a_h, a_l = split2(attended)
    inner = dot(jnp.concatenate([a_h, a_h, a_l], axis=1), chan)
    a_buf[p] = inner.astype(BF16)

    pl.semaphore_wait(barrier, NP - 1 + 8 + 1)
    def a_copy(n, m):
        return pltpu.make_async_remote_copy(
            a_buf.at[p], a_buf.at[p], a_ss.at[n * 4 + m], a_rs.at[n * 4 + m], plane(n, m), MESH
        )

    for n, m in FAR[:4]:
        a_copy(n, m).start()
    for n in (4, 12):
        pl.semaphore_signal(far_sem, inc=1, device_id=along(n), device_id_type=MESH)
    for n, m in FAR[4:]:
        a_copy(n, m).start()

    loads[-1].wait()

    @pl.loop(0, 16)
    def _(t):
        turned = w_v[:, pl.ds(pl.multiple_of(t * 128, 128), 128)].astype(F32).T.astype(BF16)
        for n in range(8):
            start = pl.multiple_of(t // 4 * 256 + (t % 4 * 4 + n // 2) * 16, 16)
            wt[pl.ds(start, 16), n % 2 * 256 : n % 2 * 256 + 256] = turned[n * 16 : n * 16 + 16, :]

    for n, m in NEAR:
        a_copy(n, m).wait_recv()

    held = a_buf[...].reshape(NP * 16, HD)
    b_send[...] = dot(kron[...], jnp.concatenate([held, held], axis=0)).astype(BF16).reshape(NZ, 16, HD)
    pl.semaphore_wait(far_sem, 2)

    def b_copy(n):
        to = (zz + n) % 16
        return pltpu.make_async_remote_copy(
            b_send.at[to // 4], b_buf.at[zz], b_ss.at[n], b_rs.at[n], along(n), MESH
        )

    for n in FAR_Z:
        b_copy(n).start()
    b_buf[zz] = b_send[z]
    for n in reversed(FAR_Z):
        b_copy(n).wait_recv()
    mixed = b_buf[0:4].astype(F32)
    for n in range(1, NZ):
        mixed = mixed + b_buf[n * 4 : n * 4 + 4].astype(F32)

    for h in range(HEADS):
        m_buf[h, :, c] = mixed[:, h * 8 : h * 8 + 8, :]
    swap = pltpu.make_async_remote_copy(m_buf.at[:, :, c], m_buf.at[:, :, c], d_ss.at[0], d_rs.at[0], sibling, MESH)
    swap.start()
    swap.wait_recv()

    rows = jnp.concatenate([m_buf[h].reshape(DP * ROWS, HD).astype(BF16) for h in range(HEADS)], axis=1)
    none = jnp.zeros_like(rows)
    both = jnp.concatenate(
        [jnp.concatenate([rows, none], axis=1), jnp.concatenate([none, rows], axis=1)], axis=0
    )

    def o_copy(part, to, origin):
        at = pl.ds(0, 1) if part == 0 else pl.ds(1, 3)
        return pltpu.make_async_remote_copy(
            o_send.at[to, at], o_buf.at[p, at], o_ss.at[part, to], o_rs.at[part, origin], (j, z * NP + to), MESH
        )

    def o_wait(part, origin):
        at = pl.ds(0, 1) if part == 0 else pl.ds(1, 3)
        pltpu.make_async_remote_copy(
            o_send.at[0, at], o_buf.at[origin, at], o_ss.at[part, 0], o_rs.at[part, origin], plane(1, 0), MESH
        ).wait_recv()

    def e_copy(to):
        return pltpu.make_async_remote_copy(o_send.at[to, 0], e_buf.at[p], e_ss.at[to], e_rs.at[p], (j, to), MESH)

    def e_wait(origin):
        pltpu.make_async_remote_copy(
            o_send.at[0, 0], e_buf.at[origin], e_ss.at[0], e_rs.at[origin], plane(1, 0), MESH
        ).wait_recv()

    straight = jnp.logical_and(z == 2, zz % 4 < 2)
    for some, peers in (((0, 64), FIRST[:4]), ((64, 256), FIRST[4:])):
        part = dot_nt(wt[some[0] : some[1], :], both).astype(BF16)
        o_send[some[0] // 16 : some[1] // 16, 0] = part.reshape((some[1] - some[0]) // 16, 16, 128)

        @pl.when(straight)
        def _(peers=peers):
            for to in peers:
                e_copy(to).start()

        @pl.when(jnp.logical_not(straight))
        def _(peers=peers):
            for to in peers:

                @pl.when(p != to)
                def _(to=to):
                    o_copy(0, to, p).start()

    for k in range(1, NZ):
        o_send[:, k] = dot_nt(wt[k * 256 : k * 256 + 256, :], both).astype(BF16).reshape(NP, 16, 128)
    for n, m in FAR:
        o_copy(1, (x + n) % 4 * 4 + (y + m) % 4, p).start()

    def f_copy(to):
        return pltpu.make_async_remote_copy(
            f_send.at[to], f_buf.at[z], f_ss.at[to], f_rs.at[z], (j, to * NP + p), MESH
        )

    def f_wait(origin):
        pltpu.make_async_remote_copy(
            f_send.at[0], f_buf.at[origin], f_ss.at[0], f_rs.at[origin], (j, (z + 1) % NZ * NP + p), MESH
        ).wait_recv()

    def source(n, m):
        return (x + 4 - n) % 4 * 4 + (y + 4 - m) % 4

    @pl.when(jnp.logical_not(straight))
    def _():
        total = o_send[p, 0].astype(F32)
        for n, m in NEAR:
            o_wait(0, source(n, m))
            total = total + o_buf[source(n, m), 0].astype(F32)
        t_buf[0] = total
        f_send[0] = total.astype(BF16)

        @pl.when(z > 0)
        def _():
            f_copy(0).start()

    totals = o_send[p, 1:4].astype(F32)
    for n, m in NEAR:
        o_wait(1, source(n, m))
        totals = totals + o_buf[source(n, m), 1:4].astype(F32)
    t_buf[1:4] = totals
    f_send[1:4] = totals.astype(BF16)
    for n in (2, 1, 3):
        to = (z + n) % NZ

        @pl.when(to > 0)
        def _(to=to):
            f_copy(to).start()

    for n, m in FAR:
        a_copy(n, m).wait_send()
        o_copy(1, (x + n) % 4 * 4 + (y + m) % 4, p).wait_send()

    @pl.when(straight)
    def _():
        for to in FIRST:
            e_copy(to).wait_send()

    @pl.when(jnp.logical_not(straight))
    def _():
        for n, m in FAR:
            o_copy(0, (x + n) % 4 * 4 + (y + m) % 4, p).wait_send()

    for n in FAR_Z:
        b_copy(n).wait_send()
    swap.wait_send()

    t_buf[NZ] = t_buf[z]
    for n in (1, 3):
        f_wait((z + n) % NZ)
        t_buf[NZ] += f_buf[(z + n) % NZ].astype(F32)

    @pl.when(zz < 2)
    def _():
        extra = jnp.zeros((16, 128), F32)
        for n, m in [(0, 0)] + NEAR:
            e_wait(source(n, m))
            extra = extra + e_buf[source(n, m)].astype(F32)
        t_buf[NZ] += extra

    @pl.when(zz >= 2)
    def _():
        f_wait((z + 2) % NZ)
        t_buf[NZ] += f_buf[(z + 2) % NZ].astype(F32)

    result = t_buf[NZ]
    result = jnp.concatenate([result[:, :64], result[:, 64:]], axis=0)
    out_ref[...] = (res_v[...].astype(F32) + result).astype(BF16)

    for to in range(NZ):
        moved = jnp.logical_and(z != to, jnp.logical_not(straight)) if to == 0 else z != to

        @pl.when(moved)
        def _(to=to):
            f_copy(to).wait_send()


def local(
    queries, cache_keys, cache_values, new_keys, new_values, key_index, value_index, scale_table, lengths,
    head_mix, channel_mix, out_weight, residual,
):
    vmem, dma = pltpu.VMEM, pltpu.SemaphoreType.DMA
    turned = pl.pallas_call(
        kernel,
        out_shape=pltpu.VMEM((32, 64), BF16),
        in_specs=[pl.BlockSpec(memory_space=pl.ANY)] * 13,
        out_specs=pl.BlockSpec(memory_space=pltpu.VMEM),
        scratch_shapes=[
            vmem((SEQ, STEPS, HEADS, HD), BF16),
            vmem((SEQ, CACHE, HD), BF16),
            vmem((SEQ, CACHE, HD), BF16),
            vmem((SEQ, STEPS, HD), BF16),
            vmem((SEQ, STEPS, HD), BF16),
            vmem((1, HD), jnp.int32),
            vmem((1, HD), jnp.int32),
            pltpu.SMEM((16,), F32),
            pltpu.SMEM((SEQ,), jnp.int32),
            vmem((128, 128), F32),
            vmem((128, 128), F32),
            vmem((256, 2048), BF16),
            vmem((32, 64), BF16),
            vmem((1024, 512), BF16),
            vmem((64, 512), BF16),
            vmem((NP, 16, HD), BF16),
            vmem((NZ, 16, HD), BF16),
            vmem((16, 16, HD), BF16),
            vmem((HEADS, 4, 2, ROWS, HD), F32),
            vmem((NP, NZ, 16, 128), BF16),
            vmem((NP, NZ, 16, 128), BF16),
            vmem((NP, 16, 128), BF16),
            vmem((NZ + 1, 16, 128), F32),
            vmem((NZ, 16, 128), BF16),
            vmem((NZ, 16, 128), BF16),
            dma((11,)),
            dma((SEQ,)),
            dma((SEQ,)),
            pltpu.SemaphoreType.REGULAR,
            dma((NP,)), dma((NP,)),
            dma((16,)), dma((16,)),
            dma((1,)), dma((1,)),
            dma((2, NP)), dma((2, NP)),
            dma((NP,)), dma((NP,)),
            dma((NZ,)), dma((NZ,)),
        ],
        compiler_params=pltpu.CompilerParams(
            collective_id=0, has_side_effects=True, vmem_limit_bytes=60 * 1024 * 1024
        ),
    )(
        queries,
        cache_keys.reshape(SEQ, CACHE, HD),
        cache_values.reshape(SEQ, CACHE, HD),
        new_keys.reshape(SEQ, STEPS, HD),
        new_values.reshape(SEQ, STEPS, HD),
        key_index, value_index, scale_table, lengths, head_mix, channel_mix, out_weight, residual.T,
    )
    return turned.T


def solution(mesh):
    in_specs = (
        P("dp", None, "head", None),
        P("dp", None, "head", None),
        P("dp", None, "head", None),
        P("dp", None, "head", None),
        P("dp", None, "head", None),
        P("head", None),
        P("head", None),
        P(),
        P("dp"),
        P(),
        P(),
        P("head", "dp"),
        P(None, ("dp", "head")),
    )
    out_specs = P(None, ("dp", "head"))
    return jax.shard_map(local, mesh=mesh, in_specs=in_specs, out_specs=out_specs, check_vma=False)
```

```python
import functools

import jax
import jax.numpy as jnp
from jax import lax
from jax.experimental import pallas as pl
from jax.experimental.pallas import tpu as pltpu
from jax.sharding import PartitionSpec as P

MESH = pl.DeviceIdType.MESH
F32, BF16 = jnp.float32, jnp.bfloat16
DP, NZ, NP = 8, 4, 16
SEQ, STEPS, HEADS, HD, CACHE = 4, 2, 2, 128, 1024
ROWS = SEQ * STEPS
FAR = [(n, m) for n in (2, 1, 3, 0) for m in (2, 1, 3, 0) if n or m]
NEAR = sorted(FAR, key=lambda at: min(at[0], 4 - at[0]) + min(at[1], 4 - at[1]))
FIRST = (0, 1, 2, 3, 4, 8, 12, 5, 6, 7, 9, 10, 11, 13, 14, 15)
FAR_Z = (8, 7, 9, 6, 10, 5, 11, 4, 12, 3, 13, 2, 14, 1, 15)
NT = (((1,), (1,)), ((), ()))


def split2(x):
    high = x.astype(BF16)
    return high, (x - high.astype(F32)).astype(BF16)


def dot(a, b):
    return jnp.dot(a, b, preferred_element_type=F32)


def dot_nt(a, b):
    return lax.dot_general(a, b, NT, preferred_element_type=F32)


def kernel(
    q_hbm, k_hbm, v_hbm, nk_hbm, nv_hbm, ki_hbm, vi_hbm, tab_hbm, len_hbm, hm_hbm, cm_hbm, w_hbm, res_hbm,
    out_ref,
    q_v, k_v, v_v, nk_v, nv_v, ki_v, vi_v, tab_s, len_s, hm_v, cm_v, w_v, res_v,
    wt, kron, a_buf, b_send, b_buf, m_buf, o_send, o_buf, e_buf, t_buf, f_send, f_buf,
    in_sem, k_sem, v_sem, far_sem, pair_sem,
    a_ss, a_rs, b_ss, b_rs, g_ss, g_rs, d_ss, d_rs, o_ss, o_rs, e_ss, e_rs, f_ss, f_rs,
):
    j = lax.axis_index("dp")
    i = lax.axis_index("head")
    c = j % 2
    z = i // NP
    zz = z * 4 + j // 2
    p = i % NP
    x = p // 4
    y = p % 4

    barrier = pltpu.get_barrier_semaphore()

    def hello(device):
        pl.semaphore_signal(barrier, inc=1, device_id=device, device_id_type=MESH)

    def along(n):
        to = (zz + n) % 16
        return to % 4 * 2 + c, to // 4 * NP + p

    def plane(n, m):
        return j, z * NP + (x + n) % 4 * 4 + (y + m) % 4

    sibling = (j + 1 - 2 * c, i)
    for n, m in FAR:
        hello(plane(n, m))
    for n in (4, 12, 3, 13, 2, 14, 1, 15):
        hello(along(n))
    hello(sibling)

    small = [
        (hm_hbm, hm_v), (cm_hbm, cm_v), (q_hbm, q_v), (ki_hbm, ki_v), (tab_hbm, tab_s), (len_hbm, len_s),
        (nk_hbm, nk_v), (nv_hbm, nv_v), (vi_hbm, vi_v), (res_hbm, res_v), (w_hbm, w_v),
    ]
    loads = [pltpu.make_async_copy(a, b, in_sem.at[n]) for n, (a, b) in enumerate(small)]
    k_loads = [pltpu.make_async_copy(k_hbm.at[s], k_v.at[s], k_sem.at[s]) for s in range(SEQ)]
    v_loads = [pltpu.make_async_copy(v_hbm.at[s], v_v.at[s], v_sem.at[s]) for s in range(SEQ)]
    for load in loads[:-1] + k_loads + v_loads:
        load.start()
    loads[-1].start()

    for load in loads[:2]:
        load.wait()

    m_row = lax.broadcasted_iota(jnp.int32, (NZ * 16, 128), 0)
    m_col = lax.broadcasted_iota(jnp.int32, (NZ * 16, 128), 1)
    pick_h = (m_col == m_row // 16 * 32 + p * 2 + m_row // 8 % 2).astype(F32)
    g_row = lax.broadcasted_iota(jnp.int32, (128, NP * 16), 0)
    g_col = lax.broadcasted_iota(jnp.int32, (128, NP * 16), 1)
    pick_g = (g_row == z * 32 + g_col // 8).astype(F32)
    wide = lax.dot_general(pick_h, hm_v[...], NT, precision=lax.Precision.HIGHEST, preferred_element_type=F32)
    wide = jnp.dot(wide, pick_g, precision=lax.Precision.HIGHEST, preferred_element_type=F32)
    a_row = lax.broadcasted_iota(jnp.int32, (NZ * 16, NP * 16), 0)
    a_col = lax.broadcasted_iota(jnp.int32, (NZ * 16, NP * 16), 1)
    wide = jnp.where(a_row % 8 == a_col % 8, wide, 0.0)
    wide_h, wide_l = split2(wide)
    kron[...] = jnp.concatenate([wide_h, wide_l], axis=1)
    c_h, c_l = split2(cm_v[...])
    chan = jnp.concatenate([c_h, c_l, c_h], axis=0)

    for load in loads[2:-1]:
        load.wait()
    key_scale = jnp.zeros((1, HD), F32)
    value_scale = jnp.zeros((1, HD), F32)
    for n in range(16):
        key_scale = jnp.where(ki_v[...] == n, tab_s[n], key_scale)
        value_scale = jnp.where(vi_v[...] == n, tab_s[n], value_scale)
    q_all = q_v[...].astype(F32)
    q = jnp.concatenate(
        [q_all[s, t, h : h + 1, :] for h in range(HEADS) for s in range(SEQ) for t in range(STEPS)], axis=0
    )
    scaled = (q * key_scale).astype(BF16)
    q_b = q.astype(BF16)
    nk_all = nk_v[...].astype(F32)
    nv_all = nv_v[...].astype(F32)
    nk = jnp.concatenate([nk_all[s] for s in range(SEQ)], axis=0).astype(BF16)
    nv = jnp.concatenate([nv_all[s] for s in range(SEQ)], axis=0).astype(BF16)

    row = lax.broadcasted_iota(jnp.int32, (16, CACHE), 0)
    row_seq = row % 8 // 2
    score = jnp.zeros((16, CACHE), F32)
    length = jnp.zeros((16, CACHE), jnp.int32)
    for s in range(SEQ):
        k_loads[s].wait()
        score = jnp.where(row_seq == s, dot_nt(scaled, k_v[s]), score)
        length = jnp.where(row_seq == s, len_s[s], length)
    inverse = 1.0 / HD**0.5
    place = lax.broadcasted_iota(jnp.int32, (16, CACHE), 1)
    score = jnp.where(place < length, score * inverse, -jnp.inf)
    new_row = lax.broadcasted_iota(jnp.int32, (16, 8), 0)
    new_col = lax.broadcasted_iota(jnp.int32, (16, 8), 1)
    seen = (new_row % 8 // 2 == new_col // 2) & (new_col % 2 <= new_row % 2)
    new_score = jnp.where(seen, dot_nt(q_b, nk) * inverse, -jnp.inf)
    top = jnp.maximum(jnp.max(score, axis=1, keepdims=True), jnp.max(new_score, axis=1, keepdims=True))
    weight = jnp.exp(score - top)
    new_weight = jnp.exp(new_score - top)
    total = jnp.sum(weight, axis=1, keepdims=True) + jnp.sum(new_weight, axis=1, keepdims=True)
    weight = weight.astype(BF16)
    attended = jnp.zeros((16, HD), F32)
    for s in range(SEQ):
        v_loads[s].wait()
        attended = jnp.where(row_seq[:, :HD] == s, dot(weight, v_v[s]), attended)
    attended = (attended * value_scale + dot(new_weight.astype(BF16), nv)) / total
    a_h, a_l = split2(attended)
    inner = dot(jnp.concatenate([a_h, a_h, a_l], axis=1), chan)
    a_buf[p] = inner.astype(BF16)

    pl.semaphore_wait(barrier, NP - 1 + 8 + 1)
    def a_copy(n, m):
        return pltpu.make_async_remote_copy(
            a_buf.at[p], a_buf.at[p], a_ss.at[n * 4 + m], a_rs.at[n * 4 + m], plane(n, m), MESH
        )

    for n, m in FAR[:4]:
        a_copy(n, m).start()
    for n in (4, 12):
        pl.semaphore_signal(far_sem, inc=1, device_id=along(n), device_id_type=MESH)
    for n, m in FAR[4:]:
        a_copy(n, m).start()

    loads[-1].wait()

    @pl.loop(0, 16)
    def _(t):
        turned = w_v[:, pl.ds(pl.multiple_of(t * 128, 128), 128)].astype(F32).T.astype(BF16)
        for n in range(8):
            start = pl.multiple_of(t // 4 * 256 + (t % 4 * 4 + n // 2) * 16, 16)
            wt[pl.ds(start, 16), n % 2 * 256 : n % 2 * 256 + 256] = turned[n * 16 : n * 16 + 16, :]

    for n, m in NEAR:
        a_copy(n, m).wait_recv()

    held = a_buf[...].reshape(NP * 16, HD)
    b_send[...] = dot(kron[...], jnp.concatenate([held, held], axis=0)).astype(BF16).reshape(NZ, 16, HD)
    pl.semaphore_wait(far_sem, 2)

    def b_copy(n):
        to = (zz + n) % 16
        return pltpu.make_async_remote_copy(
            b_send.at[to // 4], b_buf.at[c, zz], b_ss.at[n], b_rs.at[n], along(n), MESH
        )

    def g_copy(n):
        to = (z + n) % NZ
        return pltpu.make_async_remote_copy(
            b_send.at[to], b_buf.at[0, zz], g_ss.at[n], g_rs.at[zz], (1, to * NP + p), MESH
        )

    def g_wait(origin):
        pltpu.make_async_remote_copy(
            b_send.at[0], b_buf.at[0, origin], g_ss.at[0], g_rs.at[origin], sibling, MESH
        ).wait_recv()

    @pl.when(c == 1)
    def _():
        pl.semaphore_signal(pair_sem, inc=1, device_id=sibling, device_id_type=MESH)

    @pl.when(c == 0)
    def _():
        pl.semaphore_wait(pair_sem, 1)
        for n in (2, 1, 3, 0):
            g_copy(n).start()

    for n in FAR_Z:
        b_copy(n).start()
    b_buf[c, zz] = b_send[z]
    for n in reversed(FAR_Z):
        b_copy(n).wait_recv()

    def mix(core):
        mixed = b_buf[core, 0:4].astype(F32)
        for n in range(1, NZ):
            mixed = mixed + b_buf[core, n * 4 : n * 4 + 4].astype(F32)
        for h in range(HEADS):
            m_buf[h, :, core] = mixed[:, h * 8 : h * 8 + 8, :]

    mix(c)
    swap = pltpu.make_async_remote_copy(m_buf.at[:, :, c], m_buf.at[:, :, c], d_ss.at[0], d_rs.at[0], sibling, MESH)
    served = jnp.logical_and(zz % 4 == 0, c == 1)
    sends = jnp.logical_or(zz % 4 != 0, c == 1)

    @pl.when(sends)
    def _():
        swap.start()

    @pl.when(jnp.logical_not(served))
    def _():
        swap.wait_recv()

    @pl.when(served)
    def _():
        for n in range(16):
            g_wait(n)
        mix(0)

    rows = jnp.concatenate([m_buf[h].reshape(DP * ROWS, HD).astype(BF16) for h in range(HEADS)], axis=1)
    none = jnp.zeros_like(rows)
    both = jnp.concatenate(
        [jnp.concatenate([rows, none], axis=1), jnp.concatenate([none, rows], axis=1)], axis=0
    )

    def o_copy(part, to, origin):
        at = pl.ds(0, 1) if part == 0 else pl.ds(1, 3)
        return pltpu.make_async_remote_copy(
            o_send.at[to, at], o_buf.at[p, at], o_ss.at[part, to], o_rs.at[part, origin], (j, z * NP + to), MESH
        )

    def o_wait(part, origin):
        at = pl.ds(0, 1) if part == 0 else pl.ds(1, 3)
        pltpu.make_async_remote_copy(
            o_send.at[0, at], o_buf.at[origin, at], o_ss.at[part, 0], o_rs.at[part, origin], plane(1, 0), MESH
        ).wait_recv()

    def e_copy(to):
        return pltpu.make_async_remote_copy(o_send.at[to, 0], e_buf.at[p], e_ss.at[to], e_rs.at[p], (j, to), MESH)

    def e_wait(origin):
        pltpu.make_async_remote_copy(
            o_send.at[0, 0], e_buf.at[origin], e_ss.at[0], e_rs.at[origin], plane(1, 0), MESH
        ).wait_recv()

    straight = jnp.logical_and(z == 2, zz % 4 < 3)
    for some, peers in (((0, 64), FIRST[:4]), ((64, 256), FIRST[4:])):
        part = dot_nt(wt[some[0] : some[1], :], both).astype(BF16)
        o_send[some[0] // 16 : some[1] // 16, 0] = part.reshape((some[1] - some[0]) // 16, 16, 128)

        @pl.when(straight)
        def _(peers=peers):
            for to in peers:
                e_copy(to).start()

        @pl.when(jnp.logical_not(straight))
        def _(peers=peers):
            for to in peers:

                @pl.when(p != to)
                def _(to=to):
                    o_copy(0, to, p).start()

    for k in range(1, NZ):
        o_send[:, k] = dot_nt(wt[k * 256 : k * 256 + 256, :], both).astype(BF16).reshape(NP, 16, 128)
    for n, m in FAR:
        o_copy(1, (x + n) % 4 * 4 + (y + m) % 4, p).start()

    def f_copy(to):
        return pltpu.make_async_remote_copy(
            f_send.at[to], f_buf.at[z], f_ss.at[to], f_rs.at[z], (j, to * NP + p), MESH
        )

    def f_wait(origin):
        pltpu.make_async_remote_copy(
            f_send.at[0], f_buf.at[origin], f_ss.at[0], f_rs.at[origin], (j, (z + 1) % NZ * NP + p), MESH
        ).wait_recv()

    def source(n, m):
        return (x + 4 - n) % 4 * 4 + (y + 4 - m) % 4

    @pl.when(jnp.logical_not(straight))
    def _():
        total = o_send[p, 0].astype(F32)
        for n, m in NEAR:
            o_wait(0, source(n, m))
            total = total + o_buf[source(n, m), 0].astype(F32)
        t_buf[0] = total
        f_send[0] = total.astype(BF16)

        @pl.when(z > 0)
        def _():
            f_copy(0).start()

    totals = o_send[p, 1:4].astype(F32)
    for n, m in NEAR:
        o_wait(1, source(n, m))
        totals = totals + o_buf[source(n, m), 1:4].astype(F32)
    t_buf[1:4] = totals
    f_send[1:4] = totals.astype(BF16)
    for n in (2, 1, 3):
        to = (z + n) % NZ

        @pl.when(to > 0)
        def _(to=to):
            f_copy(to).start()

    for n, m in FAR:
        a_copy(n, m).wait_send()
        o_copy(1, (x + n) % 4 * 4 + (y + m) % 4, p).wait_send()

    @pl.when(straight)
    def _():
        for to in FIRST:
            e_copy(to).wait_send()

    @pl.when(jnp.logical_not(straight))
    def _():
        for n, m in FAR:
            o_copy(0, (x + n) % 4 * 4 + (y + m) % 4, p).wait_send()

    for n in FAR_Z:
        b_copy(n).wait_send()

    @pl.when(sends)
    def _():
        swap.wait_send()

    @pl.when(c == 0)
    def _():
        for n in range(NZ):
            g_copy(n).wait_send()


    t_buf[NZ] = t_buf[z]
    for n in (1, 3):
        f_wait((z + n) % NZ)
        t_buf[NZ] += f_buf[(z + n) % NZ].astype(F32)

    @pl.when(zz < 3)
    def _():
        extra = jnp.zeros((16, 128), F32)
        for n, m in [(0, 0)] + NEAR:
            e_wait(source(n, m))
            extra = extra + e_buf[source(n, m)].astype(F32)
        t_buf[NZ] += extra

    @pl.when(zz >= 3)
    def _():
        f_wait((z + 2) % NZ)
        t_buf[NZ] += f_buf[(z + 2) % NZ].astype(F32)

    result = t_buf[NZ]
    result = jnp.concatenate([result[:, :64], result[:, 64:]], axis=0)
    out_ref[...] = (res_v[...].astype(F32) + result).astype(BF16)

    for to in range(NZ):
        moved = jnp.logical_and(z != to, jnp.logical_not(straight)) if to == 0 else z != to

        @pl.when(moved)
        def _(to=to):
            f_copy(to).wait_send()


def local(
    queries, cache_keys, cache_values, new_keys, new_values, key_index, value_index, scale_table, lengths,
    head_mix, channel_mix, out_weight, residual,
):
    vmem, dma = pltpu.VMEM, pltpu.SemaphoreType.DMA
    turned = pl.pallas_call(
        kernel,
        out_shape=pltpu.VMEM((32, 64), BF16),
        in_specs=[pl.BlockSpec(memory_space=pl.ANY)] * 13,
        out_specs=pl.BlockSpec(memory_space=pltpu.VMEM),
        scratch_shapes=[
            vmem((SEQ, STEPS, HEADS, HD), BF16),
            vmem((SEQ, CACHE, HD), BF16),
            vmem((SEQ, CACHE, HD), BF16),
            vmem((SEQ, STEPS, HD), BF16),
            vmem((SEQ, STEPS, HD), BF16),
            vmem((1, HD), jnp.int32),
            vmem((1, HD), jnp.int32),
            pltpu.SMEM((16,), F32),
            pltpu.SMEM((SEQ,), jnp.int32),
            vmem((128, 128), F32),
            vmem((128, 128), F32),
            vmem((256, 2048), BF16),
            vmem((32, 64), BF16),
            vmem((1024, 512), BF16),
            vmem((64, 512), BF16),
            vmem((NP, 16, HD), BF16),
            vmem((NZ, 16, HD), BF16),
            vmem((2, 16, 16, HD), BF16),
            vmem((HEADS, 4, 2, ROWS, HD), F32),
            vmem((NP, NZ, 16, 128), BF16),
            vmem((NP, NZ, 16, 128), BF16),
            vmem((NP, 16, 128), BF16),
            vmem((NZ + 1, 16, 128), F32),
            vmem((NZ, 16, 128), BF16),
            vmem((NZ, 16, 128), BF16),
            dma((11,)),
            dma((SEQ,)),
            dma((SEQ,)),
            pltpu.SemaphoreType.REGULAR,
            pltpu.SemaphoreType.REGULAR,
            dma((NP,)), dma((NP,)),
            dma((16,)), dma((16,)),
            dma((NZ,)), dma((16,)),
            dma((1,)), dma((1,)),
            dma((2, NP)), dma((2, NP)),
            dma((NP,)), dma((NP,)),
            dma((NZ,)), dma((NZ,)),
        ],
        compiler_params=pltpu.CompilerParams(
            collective_id=0, has_side_effects=True, vmem_limit_bytes=60 * 1024 * 1024
        ),
    )(
        queries,
        cache_keys.reshape(SEQ, CACHE, HD),
        cache_values.reshape(SEQ, CACHE, HD),
        new_keys.reshape(SEQ, STEPS, HD),
        new_values.reshape(SEQ, STEPS, HD),
        key_index, value_index, scale_table, lengths, head_mix, channel_mix, out_weight, residual.T,
    )
    return turned.T


def solution(mesh):
    in_specs = (
        P("dp", None, "head", None),
        P("dp", None, "head", None),
        P("dp", None, "head", None),
        P("dp", None, "head", None),
        P("dp", None, "head", None),
        P("head", None),
        P("head", None),
        P(),
        P("dp"),
        P(),
        P(),
        P("head", "dp"),
        P(None, ("dp", "head")),
    )
    out_specs = P(None, ("dp", "head"))
    return jax.shard_map(local, mesh=mesh, in_specs=in_specs, out_specs=out_specs, check_vma=False)
```

```python
import functools

import jax
import jax.numpy as jnp
from jax import lax
from jax.experimental import pallas as pl
from jax.experimental.pallas import tpu as pltpu
from jax.sharding import PartitionSpec as P

MESH = pl.DeviceIdType.MESH
F32, BF16 = jnp.float32, jnp.bfloat16
DP, NZ, NP = 8, 4, 16
SEQ, STEPS, HEADS, HD, CACHE = 4, 2, 2, 128, 1024
ROWS = SEQ * STEPS
FAR = [(n, m) for n in (2, 1, 3, 0) for m in (2, 1, 3, 0) if n or m]
NEAR = sorted(FAR, key=lambda at: min(at[0], 4 - at[0]) + min(at[1], 4 - at[1]))
FIRST = (0, 1, 2, 3, 4, 8, 12, 5, 6, 7, 9, 10, 11, 13, 14, 15)
FAR_Z = (8, 7, 9, 6, 10, 5, 11, 4, 12, 3, 13, 2, 14, 1, 15)
NT = (((1,), (1,)), ((), ()))


def split2(x):
    high = x.astype(BF16)
    return high, (x - high.astype(F32)).astype(BF16)


def dot(a, b):
    return jnp.dot(a, b, preferred_element_type=F32)


def dot_nt(a, b):
    return lax.dot_general(a, b, NT, preferred_element_type=F32)


def kernel(
    q_hbm, k_hbm, v_hbm, nk_hbm, nv_hbm, ki_hbm, vi_hbm, tab_hbm, len_hbm, hm_hbm, cm_hbm, w_hbm, res_hbm,
    out_ref,
    q_v, k_v, v_v, nk_v, nv_v, ki_v, vi_v, tab_s, len_s, hm_v, cm_v, w_v, res_v,
    wt, kron, a_buf, b_send, b_buf, m_buf, o_send, o_buf, e_buf, t_buf, f_send, f_buf,
    in_sem, k_sem, v_sem, far_sem, pair_sem,
    a_ss, a_rs, b_ss, b_rs, g_ss, g_rs, d_ss, d_rs, o_ss, o_rs, e_ss, e_rs, f_ss, f_rs,
):
    j = lax.axis_index("dp")
    i = lax.axis_index("head")
    c = j % 2
    z = i // NP
    zz = z * 4 + j // 2
    p = i % NP
    x = p // 4
    y = p % 4

    barrier = pltpu.get_barrier_semaphore()

    def hello(device):
        pl.semaphore_signal(barrier, inc=1, device_id=device, device_id_type=MESH)

    def along(n):
        to = (zz + n) % 16
        return to % 4 * 2 + c, to // 4 * NP + p

    def plane(n, m):
        return j, z * NP + (x + n) % 4 * 4 + (y + m) % 4

    sibling = (j + 1 - 2 * c, i)
    for n, m in FAR:
        hello(plane(n, m))
    for n in (4, 12, 3, 13, 2, 14, 1, 15):
        hello(along(n))
    hello(sibling)

    small = [
        (hm_hbm, hm_v), (cm_hbm, cm_v), (q_hbm, q_v), (ki_hbm, ki_v), (tab_hbm, tab_s), (len_hbm, len_s),
        (nk_hbm, nk_v), (nv_hbm, nv_v), (vi_hbm, vi_v), (res_hbm, res_v), (w_hbm, w_v),
    ]
    loads = [pltpu.make_async_copy(a, b, in_sem.at[n]) for n, (a, b) in enumerate(small)]
    k_loads = [pltpu.make_async_copy(k_hbm.at[s], k_v.at[s], k_sem.at[s]) for s in range(SEQ)]
    v_loads = [pltpu.make_async_copy(v_hbm.at[s], v_v.at[s], v_sem.at[s]) for s in range(SEQ)]
    for load in loads[:-1] + k_loads + v_loads:
        load.start()
    loads[-1].start()

    for load in loads[:2]:
        load.wait()

    m_row = lax.broadcasted_iota(jnp.int32, (NZ * 16, 128), 0)
    m_col = lax.broadcasted_iota(jnp.int32, (NZ * 16, 128), 1)
    pick_h = (m_col == m_row // 16 * 32 + p * 2 + m_row // 8 % 2).astype(F32)
    g_row = lax.broadcasted_iota(jnp.int32, (128, NP * 16), 0)
    g_col = lax.broadcasted_iota(jnp.int32, (128, NP * 16), 1)
    pick_g = (g_row == z * 32 + g_col // 8).astype(F32)
    wide = lax.dot_general(pick_h, hm_v[...], NT, precision=lax.Precision.HIGHEST, preferred_element_type=F32)
    wide = jnp.dot(wide, pick_g, precision=lax.Precision.HIGHEST, preferred_element_type=F32)
    a_row = lax.broadcasted_iota(jnp.int32, (NZ * 16, NP * 16), 0)
    a_col = lax.broadcasted_iota(jnp.int32, (NZ * 16, NP * 16), 1)
    wide = jnp.where(a_row % 8 == a_col % 8, wide, 0.0)
    wide_h, wide_l = split2(wide)
    kron[...] = jnp.concatenate([wide_h, wide_l], axis=0)
    c_h, c_l = split2(cm_v[...])
    chan = jnp.concatenate([c_h, c_l, c_h], axis=0)

    for load in loads[2:-1]:
        load.wait()
    key_scale = jnp.zeros((1, HD), F32)
    value_scale = jnp.zeros((1, HD), F32)
    for n in range(16):
        key_scale = jnp.where(ki_v[...] == n, tab_s[n], key_scale)
        value_scale = jnp.where(vi_v[...] == n, tab_s[n], value_scale)
    q_all = q_v[...].astype(F32)
    q = jnp.concatenate(
        [q_all[s, t, h : h + 1, :] for h in range(HEADS) for s in range(SEQ) for t in range(STEPS)], axis=0
    )
    scaled = (q * key_scale).astype(BF16)
    q_b = q.astype(BF16)
    nk_all = nk_v[...].astype(F32)
    nv_all = nv_v[...].astype(F32)
    nk = jnp.concatenate([nk_all[s] for s in range(SEQ)], axis=0).astype(BF16)
    nv = jnp.concatenate([nv_all[s] for s in range(SEQ)], axis=0).astype(BF16)

    row = lax.broadcasted_iota(jnp.int32, (16, CACHE), 0)
    row_seq = row % 8 // 2
    score = jnp.zeros((16, CACHE), F32)
    length = jnp.zeros((16, CACHE), jnp.int32)
    for s in range(SEQ):
        k_loads[s].wait()
        score = jnp.where(row_seq == s, dot_nt(scaled, k_v[s]), score)
        length = jnp.where(row_seq == s, len_s[s], length)
    inverse = 1.0 / HD**0.5
    place = lax.broadcasted_iota(jnp.int32, (16, CACHE), 1)
    score = jnp.where(place < length, score * inverse, -jnp.inf)
    new_row = lax.broadcasted_iota(jnp.int32, (16, 8), 0)
    new_col = lax.broadcasted_iota(jnp.int32, (16, 8), 1)
    seen = (new_row % 8 // 2 == new_col // 2) & (new_col % 2 <= new_row % 2)
    new_score = jnp.where(seen, dot_nt(q_b, nk) * inverse, -jnp.inf)
    top = jnp.maximum(jnp.max(score, axis=1, keepdims=True), jnp.max(new_score, axis=1, keepdims=True))
    weight = jnp.exp(score - top)
    new_weight = jnp.exp(new_score - top)
    total = jnp.sum(weight, axis=1, keepdims=True) + jnp.sum(new_weight, axis=1, keepdims=True)
    weight = weight.astype(BF16)
    attended = jnp.zeros((16, HD), F32)
    for s in range(SEQ):
        v_loads[s].wait()
        attended = jnp.where(row_seq[:, :HD] == s, dot(weight, v_v[s]), attended)
    attended = (attended * value_scale + dot(new_weight.astype(BF16), nv)) / total
    a_h, a_l = split2(attended)
    inner = dot(jnp.concatenate([a_h, a_h, a_l], axis=1), chan)
    a_buf[p] = inner.astype(BF16)

    pl.semaphore_wait(barrier, NP - 1 + 8 + 1)
    def a_copy(n, m):
        return pltpu.make_async_remote_copy(
            a_buf.at[p], a_buf.at[p], a_ss.at[n * 4 + m], a_rs.at[n * 4 + m], plane(n, m), MESH
        )

    for n, m in FAR[:4]:
        a_copy(n, m).start()
    for n in (4, 12):
        pl.semaphore_signal(far_sem, inc=1, device_id=along(n), device_id_type=MESH)
    for n, m in FAR[4:]:
        a_copy(n, m).start()

    loads[-1].wait()

    @pl.loop(0, 16)
    def _(t):
        turned = w_v[:, pl.ds(pl.multiple_of(t * 128, 128), 128)].astype(F32).T.astype(BF16)
        for n in range(8):
            start = pl.multiple_of(t // 4 * 256 + (t % 4 * 4 + n // 2) * 16, 16)
            wt[pl.ds(start, 16), n % 2 * 256 : n % 2 * 256 + 256] = turned[n * 16 : n * 16 + 16, :]

    for n, m in NEAR:
        a_copy(n, m).wait_recv()

    held = a_buf[...].reshape(NP * 16, HD)
    shares = dot(kron[...], held)
    b_send[...] = (shares[:64] + shares[64:]).astype(BF16).reshape(NZ, 16, HD)
    pl.semaphore_wait(far_sem, 2)

    def b_copy(n):
        to = (zz + n) % 16
        return pltpu.make_async_remote_copy(
            b_send.at[to // 4], b_buf.at[c, zz], b_ss.at[n], b_rs.at[n], along(n), MESH
        )

    def g_copy(n):
        to = (z + n) % NZ
        return pltpu.make_async_remote_copy(
            b_send.at[to], b_buf.at[0, zz], g_ss.at[n], g_rs.at[zz], (1, to * NP + p), MESH
        )

    def g_wait(origin):
        pltpu.make_async_remote_copy(
            b_send.at[0], b_buf.at[0, origin], g_ss.at[0], g_rs.at[origin], sibling, MESH
        ).wait_recv()

    @pl.when(c == 1)
    def _():
        pl.semaphore_signal(pair_sem, inc=1, device_id=sibling, device_id_type=MESH)

    @pl.when(c == 0)
    def _():
        pl.semaphore_wait(pair_sem, 1)
        for n in (2, 1, 3, 0):
            g_copy(n).start()

    for n in FAR_Z:
        b_copy(n).start()
    b_buf[c, zz] = b_send[z]
    for n in reversed(FAR_Z):
        b_copy(n).wait_recv()

    def mix(core):
        mixed = b_buf[core, 0:4].astype(F32)
        for n in range(1, NZ):
            mixed = mixed + b_buf[core, n * 4 : n * 4 + 4].astype(F32)
        for h in range(HEADS):
            m_buf[h, :, core] = mixed[:, h * 8 : h * 8 + 8, :]

    mix(c)
    swap = pltpu.make_async_remote_copy(m_buf.at[:, :, c], m_buf.at[:, :, c], d_ss.at[0], d_rs.at[0], sibling, MESH)
    served = jnp.logical_and(zz % 4 == 0, c == 1)
    sends = jnp.logical_or(zz % 4 != 0, c == 1)

    @pl.when(sends)
    def _():
        swap.start()

    @pl.when(jnp.logical_not(served))
    def _():
        swap.wait_recv()

    @pl.when(served)
    def _():
        for n in range(16):
            g_wait(n)
        mix(0)

    rows = jnp.concatenate([m_buf[h].reshape(DP * ROWS, HD).astype(BF16) for h in range(HEADS)], axis=1)
    none = jnp.zeros_like(rows)
    both = jnp.concatenate(
        [jnp.concatenate([rows, none], axis=1), jnp.concatenate([none, rows], axis=1)], axis=0
    )

    def o_copy(part, to, origin):
        at = pl.ds(0, 1) if part == 0 else pl.ds(1, 3)
        return pltpu.make_async_remote_copy(
            o_send.at[to, at], o_buf.at[p, at], o_ss.at[part, to], o_rs.at[part, origin], (j, z * NP + to), MESH
        )

    def o_wait(part, origin):
        at = pl.ds(0, 1) if part == 0 else pl.ds(1, 3)
        pltpu.make_async_remote_copy(
            o_send.at[0, at], o_buf.at[origin, at], o_ss.at[part, 0], o_rs.at[part, origin], plane(1, 0), MESH
        ).wait_recv()

    def e_copy(to):
        return pltpu.make_async_remote_copy(o_send.at[to, 0], e_buf.at[p], e_ss.at[to], e_rs.at[p], (j, to), MESH)

    def e_wait(origin):
        pltpu.make_async_remote_copy(
            o_send.at[0, 0], e_buf.at[origin], e_ss.at[0], e_rs.at[origin], plane(1, 0), MESH
        ).wait_recv()

    straight = jnp.logical_and(z == 2, zz % 4 < 3)
    for some, peers in (((0, 64), FIRST[:4]), ((64, 256), FIRST[4:])):
        part = dot_nt(wt[some[0] : some[1], :], both).astype(BF16)
        o_send[some[0] // 16 : some[1] // 16, 0] = part.reshape((some[1] - some[0]) // 16, 16, 128)

        @pl.when(straight)
        def _(peers=peers):
            for to in peers:
                e_copy(to).start()

        @pl.when(jnp.logical_not(straight))
        def _(peers=peers):
            for to in peers:

                @pl.when(p != to)
                def _(to=to):
                    o_copy(0, to, p).start()

    for k in range(1, NZ):
        o_send[:, k] = dot_nt(wt[k * 256 : k * 256 + 256, :], both).astype(BF16).reshape(NP, 16, 128)
    for n, m in FAR:
        o_copy(1, (x + n) % 4 * 4 + (y + m) % 4, p).start()

    def f_copy(to):
        return pltpu.make_async_remote_copy(
            f_send.at[to], f_buf.at[z], f_ss.at[to], f_rs.at[z], (j, to * NP + p), MESH
        )

    def f_wait(origin):
        pltpu.make_async_remote_copy(
            f_send.at[0], f_buf.at[origin], f_ss.at[0], f_rs.at[origin], (j, (z + 1) % NZ * NP + p), MESH
        ).wait_recv()

    def source(n, m):
        return (x + 4 - n) % 4 * 4 + (y + 4 - m) % 4

    @pl.when(jnp.logical_not(straight))
    def _():
        total = o_send[p, 0].astype(F32)
        for n, m in NEAR:
            o_wait(0, source(n, m))
            total = total + o_buf[source(n, m), 0].astype(F32)
        t_buf[0] = total
        f_send[0] = total.astype(BF16)

        @pl.when(z > 0)
        def _():
            f_copy(0).start()

    totals = o_send[p, 1:4].astype(F32)
    for n, m in NEAR:
        o_wait(1, source(n, m))
        totals = totals + o_buf[source(n, m), 1:4].astype(F32)
    t_buf[1:4] = totals
    f_send[1:4] = totals.astype(BF16)
    for n in (2, 1, 3):
        to = (z + n) % NZ

        @pl.when(to > 0)
        def _(to=to):
            f_copy(to).start()

    for n, m in FAR:
        a_copy(n, m).wait_send()
        o_copy(1, (x + n) % 4 * 4 + (y + m) % 4, p).wait_send()

    @pl.when(straight)
    def _():
        for to in FIRST:
            e_copy(to).wait_send()

    @pl.when(jnp.logical_not(straight))
    def _():
        for n, m in FAR:
            o_copy(0, (x + n) % 4 * 4 + (y + m) % 4, p).wait_send()

    for n in FAR_Z:
        b_copy(n).wait_send()

    @pl.when(sends)
    def _():
        swap.wait_send()

    @pl.when(c == 0)
    def _():
        for n in range(NZ):
            g_copy(n).wait_send()


    t_buf[NZ] = t_buf[z]
    for n in (1, 3):
        f_wait((z + n) % NZ)
        t_buf[NZ] += f_buf[(z + n) % NZ].astype(F32)

    @pl.when(zz < 3)
    def _():
        extra = jnp.zeros((16, 128), F32)
        for n, m in [(0, 0)] + NEAR:
            e_wait(source(n, m))
            extra = extra + e_buf[source(n, m)].astype(F32)
        t_buf[NZ] += extra

    @pl.when(zz >= 3)
    def _():
        f_wait((z + 2) % NZ)
        t_buf[NZ] += f_buf[(z + 2) % NZ].astype(F32)

    result = t_buf[NZ]
    result = jnp.concatenate([result[:, :64], result[:, 64:]], axis=0)
    out_ref[...] = (res_v[...].astype(F32) + result).astype(BF16)

    for to in range(NZ):
        moved = jnp.logical_and(z != to, jnp.logical_not(straight)) if to == 0 else z != to

        @pl.when(moved)
        def _(to=to):
            f_copy(to).wait_send()


def local(
    queries, cache_keys, cache_values, new_keys, new_values, key_index, value_index, scale_table, lengths,
    head_mix, channel_mix, out_weight, residual,
):
    vmem, dma = pltpu.VMEM, pltpu.SemaphoreType.DMA
    turned = pl.pallas_call(
        kernel,
        out_shape=pltpu.VMEM((32, 64), BF16),
        in_specs=[pl.BlockSpec(memory_space=pl.ANY)] * 13,
        out_specs=pl.BlockSpec(memory_space=pltpu.VMEM),
        scratch_shapes=[
            vmem((SEQ, STEPS, HEADS, HD), BF16),
            vmem((SEQ, CACHE, HD), BF16),
            vmem((SEQ, CACHE, HD), BF16),
            vmem((SEQ, STEPS, HD), BF16),
            vmem((SEQ, STEPS, HD), BF16),
            vmem((1, HD), jnp.int32),
            vmem((1, HD), jnp.int32),
            pltpu.SMEM((16,), F32),
            pltpu.SMEM((SEQ,), jnp.int32),
            vmem((128, 128), F32),
            vmem((128, 128), F32),
            vmem((256, 2048), BF16),
            vmem((32, 64), BF16),
            vmem((1024, 512), BF16),
            vmem((128, 256), BF16),
            vmem((NP, 16, HD), BF16),
            vmem((NZ, 16, HD), BF16),
            vmem((2, 16, 16, HD), BF16),
            vmem((HEADS, 4, 2, ROWS, HD), F32),
            vmem((NP, NZ, 16, 128), BF16),
            vmem((NP, NZ, 16, 128), BF16),
            vmem((NP, 16, 128), BF16),
            vmem((NZ + 1, 16, 128), F32),
            vmem((NZ, 16, 128), BF16),
            vmem((NZ, 16, 128), BF16),
            dma((11,)),
            dma((SEQ,)),
            dma((SEQ,)),
            pltpu.SemaphoreType.REGULAR,
            pltpu.SemaphoreType.REGULAR,
            dma((NP,)), dma((NP,)),
            dma((16,)), dma((16,)),
            dma((NZ,)), dma((16,)),
            dma((1,)), dma((1,)),
            dma((2, NP)), dma((2, NP)),
            dma((NP,)), dma((NP,)),
            dma((NZ,)), dma((NZ,)),
        ],
        compiler_params=pltpu.CompilerParams(
            collective_id=0, has_side_effects=True, vmem_limit_bytes=60 * 1024 * 1024
        ),
    )(
        queries,
        cache_keys.reshape(SEQ, CACHE, HD),
        cache_values.reshape(SEQ, CACHE, HD),
        new_keys.reshape(SEQ, STEPS, HD),
        new_values.reshape(SEQ, STEPS, HD),
        key_index, value_index, scale_table, lengths, head_mix, channel_mix, out_weight, residual.T,
    )
    return turned.T


def solution(mesh):
    in_specs = (
        P("dp", None, "head", None),
        P("dp", None, "head", None),
        P("dp", None, "head", None),
        P("dp", None, "head", None),
        P("dp", None, "head", None),
        P("head", None),
        P("head", None),
        P(),
        P("dp"),
        P(),
        P(),
        P("head", "dp"),
        P(None, ("dp", "head")),
    )
    out_specs = P(None, ("dp", "head"))
    return jax.shard_map(local, mesh=mesh, in_specs=in_specs, out_specs=out_specs, check_vma=False)
```

```python
import functools

import jax
import jax.numpy as jnp
from jax import lax
from jax.experimental import pallas as pl
from jax.experimental.pallas import tpu as pltpu
from jax.sharding import PartitionSpec as P

MESH = pl.DeviceIdType.MESH
F32, BF16 = jnp.float32, jnp.bfloat16
DP, NZ, NP = 8, 4, 16
SEQ, STEPS, HEADS, HD, CACHE = 4, 2, 2, 128, 1024
ROWS = SEQ * STEPS
FAR = [(n, m) for n in (2, 1, 3, 0) for m in (2, 1, 3, 0) if n or m]
NEAR = sorted(FAR, key=lambda at: min(at[0], 4 - at[0]) + min(at[1], 4 - at[1]))
FIRST = (0, 1, 2, 3, 4, 8, 12, 5, 6, 7, 9, 10, 11, 13, 14, 15)
FAR_Z = (8, 7, 9, 6, 10, 5, 11, 4, 12, 3, 13, 2, 14, 1, 15)
NT = (((1,), (1,)), ((), ()))


def split2(x):
    high = x.astype(BF16)
    return high, (x - high.astype(F32)).astype(BF16)


def dot(a, b):
    return jnp.dot(a, b, preferred_element_type=F32)


def dot_nt(a, b):
    return lax.dot_general(a, b, NT, preferred_element_type=F32)


def kernel(
    q_hbm, k_hbm, v_hbm, nk_hbm, nv_hbm, ki_hbm, vi_hbm, tab_hbm, len_hbm, hm_hbm, cm_hbm, w_hbm, res_hbm,
    out_ref,
    q_v, k_v, v_v, nk_v, nv_v, ki_v, vi_v, tab_s, len_s, hm_v, cm_v, w_v, res_v,
    wt, kron, a_buf, b_send, b_buf, m_buf, o_send, o_buf, e_buf, t_buf, f_send, f_buf,
    in_sem, k_sem, v_sem, far_sem, pair_sem,
    a_ss, a_rs, b_ss, b_rs, g_ss, g_rs, d_ss, d_rs, o_ss, o_rs, e_ss, e_rs, f_ss, f_rs,
):
    j = lax.axis_index("dp")
    i = lax.axis_index("head")
    c = j % 2
    z = i // NP
    zz = z * 4 + j // 2
    p = i % NP
    x = p // 4
    y = p % 4

    barrier = pltpu.get_barrier_semaphore()

    def hello(device):
        pl.semaphore_signal(barrier, inc=1, device_id=device, device_id_type=MESH)

    def along(n):
        to = (zz + n) % 16
        return to % 4 * 2 + c, to // 4 * NP + p

    def plane(n, m):
        return j, z * NP + (x + n) % 4 * 4 + (y + m) % 4

    sibling = (j + 1 - 2 * c, i)
    for n, m in FAR:
        hello(plane(n, m))
    for n in (4, 12, 3, 13, 2, 14, 1, 15):
        hello(along(n))
    hello(sibling)

    small = [
        (hm_hbm, hm_v), (cm_hbm, cm_v), (q_hbm, q_v), (ki_hbm, ki_v), (tab_hbm, tab_s), (len_hbm, len_s),
        (nk_hbm, nk_v), (nv_hbm, nv_v), (vi_hbm, vi_v), (res_hbm, res_v), (w_hbm, w_v),
    ]
    loads = [pltpu.make_async_copy(a, b, in_sem.at[n]) for n, (a, b) in enumerate(small)]
    k_loads = [pltpu.make_async_copy(k_hbm.at[s], k_v.at[s], k_sem.at[s]) for s in range(SEQ)]
    v_loads = [pltpu.make_async_copy(v_hbm.at[s], v_v.at[s], v_sem.at[s]) for s in range(SEQ)]
    for load in loads[:-1] + k_loads + v_loads:
        load.start()
    loads[-1].start()

    for load in loads[:2]:
        load.wait()

    m_row = lax.broadcasted_iota(jnp.int32, (NZ * 16, 128), 0)
    m_col = lax.broadcasted_iota(jnp.int32, (NZ * 16, 128), 1)
    pick_h = (m_col == m_row // 16 * 32 + p * 2 + m_row // 8 % 2).astype(F32)
    g_row = lax.broadcasted_iota(jnp.int32, (128, NP * 16), 0)
    g_col = lax.broadcasted_iota(jnp.int32, (128, NP * 16), 1)
    pick_g = (g_row == z * 32 + g_col // 8).astype(F32)
    wide = lax.dot_general(pick_h, hm_v[...], NT, precision=lax.Precision.HIGHEST, preferred_element_type=F32)
    wide = jnp.dot(wide, pick_g, precision=lax.Precision.HIGHEST, preferred_element_type=F32)
    a_row = lax.broadcasted_iota(jnp.int32, (NZ * 16, NP * 16), 0)
    a_col = lax.broadcasted_iota(jnp.int32, (NZ * 16, NP * 16), 1)
    wide = jnp.where(a_row % 8 == a_col % 8, wide, 0.0)
    wide_h, wide_l = split2(wide)
    kron[...] = jnp.concatenate([wide_h, wide_l], axis=1)
    c_h, c_l = split2(cm_v[...])
    chan = jnp.concatenate([c_h, c_l, c_h], axis=0)

    for load in loads[2:-1]:
        load.wait()
    key_scale = jnp.zeros((1, HD), F32)
    value_scale = jnp.zeros((1, HD), F32)
    for n in range(16):
        key_scale = jnp.where(ki_v[...] == n, tab_s[n], key_scale)
        value_scale = jnp.where(vi_v[...] == n, tab_s[n], value_scale)
    q_all = q_v[...].astype(F32)
    q = jnp.concatenate(
        [q_all[s, t, h : h + 1, :] for h in range(HEADS) for s in range(SEQ) for t in range(STEPS)], axis=0
    )
    scaled = (q * key_scale).astype(BF16)
    q_b = q.astype(BF16)
    nk_all = nk_v[...].astype(F32)
    nv_all = nv_v[...].astype(F32)
    nk = jnp.concatenate([nk_all[s] for s in range(SEQ)], axis=0).astype(BF16)
    nv = jnp.concatenate([nv_all[s] for s in range(SEQ)], axis=0).astype(BF16)

    row = lax.broadcasted_iota(jnp.int32, (16, CACHE), 0)
    row_seq = row % 8 // 2
    score = jnp.zeros((16, CACHE), F32)
    length = jnp.zeros((16, CACHE), jnp.int32)
    for s in range(SEQ):
        k_loads[s].wait()
        score = jnp.where(row_seq == s, dot_nt(scaled, k_v[s]), score)
        length = jnp.where(row_seq == s, len_s[s], length)
    inverse = 1.0 / HD**0.5
    place = lax.broadcasted_iota(jnp.int32, (16, CACHE), 1)
    score = jnp.where(place < length, score * inverse, -jnp.inf)
    new_row = lax.broadcasted_iota(jnp.int32, (16, 8), 0)
    new_col = lax.broadcasted_iota(jnp.int32, (16, 8), 1)
    seen = (new_row % 8 // 2 == new_col // 2) & (new_col % 2 <= new_row % 2)
    new_score = jnp.where(seen, dot_nt(q_b, nk) * inverse, -jnp.inf)
    top = jnp.maximum(jnp.max(score, axis=1, keepdims=True), jnp.max(new_score, axis=1, keepdims=True))
    weight = jnp.exp(score - top)
    new_weight = jnp.exp(new_score - top)
    total = jnp.sum(weight, axis=1, keepdims=True) + jnp.sum(new_weight, axis=1, keepdims=True)
    weight = weight.astype(BF16)
    attended = jnp.zeros((16, HD), F32)
    for s in range(SEQ):
        v_loads[s].wait()
        attended = jnp.where(row_seq[:, :HD] == s, dot(weight, v_v[s]), attended)
    attended = (attended * value_scale + dot(new_weight.astype(BF16), nv)) / total
    a_h, a_l = split2(attended)
    inner = dot(jnp.concatenate([a_h, a_h, a_l], axis=1), chan)
    a_buf[p] = inner.astype(BF16)

    pl.semaphore_wait(barrier, NP - 1 + 8 + 1)
    def a_copy(n, m):
        return pltpu.make_async_remote_copy(
            a_buf.at[p], a_buf.at[p], a_ss.at[n * 4 + m], a_rs.at[n * 4 + m], plane(n, m), MESH
        )

    for n in (4, 12):
        pl.semaphore_signal(far_sem, inc=1, device_id=along(n), device_id_type=MESH)
    for n, m in FAR:
        a_copy(n, m).start()

    loads[-1].wait()

    @pl.loop(0, 16)
    def _(t):
        turned = w_v[:, pl.ds(pl.multiple_of(t * 128, 128), 128)].astype(F32).T.astype(BF16)
        for n in range(8):
            start = pl.multiple_of(t // 4 * 256 + (t % 4 * 4 + n // 2) * 16, 16)
            wt[pl.ds(start, 16), n % 2 * 256 : n % 2 * 256 + 256] = turned[n * 16 : n * 16 + 16, :]

    for n, m in NEAR:
        a_copy(n, m).wait_recv()

    held = a_buf[...].reshape(NP * 16, HD)
    b_send[...] = dot(kron[...], jnp.concatenate([held, held], axis=0)).astype(BF16).reshape(NZ, 16, HD)
    pl.semaphore_wait(far_sem, 2)

    def b_copy(n):
        to = (zz + n) % 16
        return pltpu.make_async_remote_copy(
            b_send.at[to // 4], b_buf.at[c, zz], b_ss.at[n], b_rs.at[n], along(n), MESH
        )

    def g_copy(n):
        to = (z + n) % NZ
        return pltpu.make_async_remote_copy(
            b_send.at[to], b_buf.at[0, zz], g_ss.at[n], g_rs.at[zz], (1, to * NP + p), MESH
        )

    def g_wait(origin):
        pltpu.make_async_remote_copy(
            b_send.at[0], b_buf.at[0, origin], g_ss.at[0], g_rs.at[origin], sibling, MESH
        ).wait_recv()

    @pl.when(c == 1)
    def _():
        pl.semaphore_signal(pair_sem, inc=1, device_id=sibling, device_id_type=MESH)

    @pl.when(c == 0)
    def _():
        pl.semaphore_wait(pair_sem, 1)
        for n in (2, 1, 3, 0):
            g_copy(n).start()

    for n in FAR_Z:
        b_copy(n).start()
    b_buf[c, zz] = b_send[z]
    for n in reversed(FAR_Z):
        b_copy(n).wait_recv()

    def mix(core):
        mixed = b_buf[core, 0:4].astype(F32)
        for n in range(1, NZ):
            mixed = mixed + b_buf[core, n * 4 : n * 4 + 4].astype(F32)
        for h in range(HEADS):
            m_buf[h, :, core] = mixed[:, h * 8 : h * 8 + 8, :]

    mix(c)
    swap = pltpu.make_async_remote_copy(m_buf.at[:, :, c], m_buf.at[:, :, c], d_ss.at[0], d_rs.at[0], sibling, MESH)
    served = jnp.logical_and(zz % 4 == 0, c == 1)
    sends = jnp.logical_or(zz % 4 != 0, c == 1)

    @pl.when(sends)
    def _():
        swap.start()

    @pl.when(jnp.logical_not(served))
    def _():
        swap.wait_recv()

    @pl.when(served)
    def _():
        for n in range(16):
            g_wait(n)
        mix(0)

    rows = jnp.concatenate([m_buf[h].reshape(DP * ROWS, HD).astype(BF16) for h in range(HEADS)], axis=1)
    none = jnp.zeros_like(rows)
    both = jnp.concatenate(
        [jnp.concatenate([rows, none], axis=1), jnp.concatenate([none, rows], axis=1)], axis=0
    )

    def o_copy(part, to, origin):
        at = pl.ds(0, 1) if part == 0 else pl.ds(1, 3)
        return pltpu.make_async_remote_copy(
            o_send.at[to, at], o_buf.at[p, at], o_ss.at[part, to], o_rs.at[part, origin], (j, z * NP + to), MESH
        )

    def o_wait(part, origin):
        at = pl.ds(0, 1) if part == 0 else pl.ds(1, 3)
        pltpu.make_async_remote_copy(
            o_send.at[0, at], o_buf.at[origin, at], o_ss.at[part, 0], o_rs.at[part, origin], plane(1, 0), MESH
        ).wait_recv()

    def e_copy(to):
        return pltpu.make_async_remote_copy(o_send.at[to, 0], e_buf.at[p], e_ss.at[to], e_rs.at[p], (j, to), MESH)

    def e_wait(origin):
        pltpu.make_async_remote_copy(
            o_send.at[0, 0], e_buf.at[origin], e_ss.at[0], e_rs.at[origin], plane(1, 0), MESH
        ).wait_recv()

    straight = jnp.logical_and(z == 2, zz % 4 < 3)
    for some, peers in (((0, 64), FIRST[:4]), ((64, 256), FIRST[4:])):
        part = dot_nt(wt[some[0] : some[1], :], both).astype(BF16)
        o_send[some[0] // 16 : some[1] // 16, 0] = part.reshape((some[1] - some[0]) // 16, 16, 128)

        @pl.when(straight)
        def _(peers=peers):
            for to in peers:
                e_copy(to).start()

        @pl.when(jnp.logical_not(straight))
        def _(peers=peers):
            for to in peers:

                @pl.when(p != to)
                def _(to=to):
                    o_copy(0, to, p).start()

    for k in range(1, NZ):
        o_send[:, k] = dot_nt(wt[k * 256 : k * 256 + 256, :], both).astype(BF16).reshape(NP, 16, 128)
    for n, m in FAR:
        o_copy(1, (x + n) % 4 * 4 + (y + m) % 4, p).start()

    def f_copy(to):
        return pltpu.make_async_remote_copy(
            f_send.at[to], f_buf.at[z], f_ss.at[to], f_rs.at[z], (j, to * NP + p), MESH
        )

    def f_wait(origin):
        pltpu.make_async_remote_copy(
            f_send.at[0], f_buf.at[origin], f_ss.at[0], f_rs.at[origin], (j, (z + 1) % NZ * NP + p), MESH
        ).wait_recv()

    def source(n, m):
        return (x + 4 - n) % 4 * 4 + (y + 4 - m) % 4

    @pl.when(jnp.logical_not(straight))
    def _():
        total = o_send[p, 0].astype(F32)
        for n, m in NEAR:
            o_wait(0, source(n, m))
            total = total + o_buf[source(n, m), 0].astype(F32)
        t_buf[0] = total
        f_send[0] = total.astype(BF16)

        @pl.when(z > 0)
        def _():
            f_copy(0).start()

    totals = o_send[p, 1:4].astype(F32)
    for n, m in NEAR:
        o_wait(1, source(n, m))
        totals = totals + o_buf[source(n, m), 1:4].astype(F32)
    t_buf[1:4] = totals
    f_send[1:4] = totals.astype(BF16)
    for n in (2, 1, 3):
        to = (z + n) % NZ

        @pl.when(to > 0)
        def _(to=to):
            f_copy(to).start()

    for n, m in FAR:
        a_copy(n, m).wait_send()
        o_copy(1, (x + n) % 4 * 4 + (y + m) % 4, p).wait_send()

    @pl.when(straight)
    def _():
        for to in FIRST:
            e_copy(to).wait_send()

    @pl.when(jnp.logical_not(straight))
    def _():
        for n, m in FAR:
            o_copy(0, (x + n) % 4 * 4 + (y + m) % 4, p).wait_send()

    for n in FAR_Z:
        b_copy(n).wait_send()

    @pl.when(sends)
    def _():
        swap.wait_send()

    @pl.when(c == 0)
    def _():
        for n in range(NZ):
            g_copy(n).wait_send()


    t_buf[NZ] = t_buf[z]
    for n in (1, 3):
        f_wait((z + n) % NZ)
        t_buf[NZ] += f_buf[(z + n) % NZ].astype(F32)

    @pl.when(zz < 3)
    def _():
        extra = jnp.zeros((16, 128), F32)
        for n, m in [(0, 0)] + NEAR:
            e_wait(source(n, m))
            extra = extra + e_buf[source(n, m)].astype(F32)
        t_buf[NZ] += extra

    @pl.when(zz >= 3)
    def _():
        f_wait((z + 2) % NZ)
        t_buf[NZ] += f_buf[(z + 2) % NZ].astype(F32)

    result = t_buf[NZ]
    result = jnp.concatenate([result[:, :64], result[:, 64:]], axis=0)
    out_ref[...] = (res_v[...].astype(F32) + result).astype(BF16)

    for to in range(NZ):
        moved = jnp.logical_and(z != to, jnp.logical_not(straight)) if to == 0 else z != to

        @pl.when(moved)
        def _(to=to):
            f_copy(to).wait_send()


def local(
    queries, cache_keys, cache_values, new_keys, new_values, key_index, value_index, scale_table, lengths,
    head_mix, channel_mix, out_weight, residual,
):
    vmem, dma = pltpu.VMEM, pltpu.SemaphoreType.DMA
    turned = pl.pallas_call(
        kernel,
        out_shape=pltpu.VMEM((32, 64), BF16),
        in_specs=[pl.BlockSpec(memory_space=pl.ANY)] * 13,
        out_specs=pl.BlockSpec(memory_space=pltpu.VMEM),
        scratch_shapes=[
            vmem((SEQ, STEPS, HEADS, HD), BF16),
            vmem((SEQ, CACHE, HD), BF16),
            vmem((SEQ, CACHE, HD), BF16),
            vmem((SEQ, STEPS, HD), BF16),
            vmem((SEQ, STEPS, HD), BF16),
            vmem((1, HD), jnp.int32),
            vmem((1, HD), jnp.int32),
            pltpu.SMEM((16,), F32),
            pltpu.SMEM((SEQ,), jnp.int32),
            vmem((128, 128), F32),
            vmem((128, 128), F32),
            vmem((256, 2048), BF16),
            vmem((32, 64), BF16),
            vmem((1024, 512), BF16),
            vmem((64, 512), BF16),
            vmem((NP, 16, HD), BF16),
            vmem((NZ, 16, HD), BF16),
            vmem((2, 16, 16, HD), BF16),
            vmem((HEADS, 4, 2, ROWS, HD), F32),
            vmem((NP, NZ, 16, 128), BF16),
            vmem((NP, NZ, 16, 128), BF16),
            vmem((NP, 16, 128), BF16),
            vmem((NZ + 1, 16, 128), F32),
            vmem((NZ, 16, 128), BF16),
            vmem((NZ, 16, 128), BF16),
            dma((11,)),
            dma((SEQ,)),
            dma((SEQ,)),
            pltpu.SemaphoreType.REGULAR,
            pltpu.SemaphoreType.REGULAR,
            dma((NP,)), dma((NP,)),
            dma((16,)), dma((16,)),
            dma((NZ,)), dma((16,)),
            dma((1,)), dma((1,)),
            dma((2, NP)), dma((2, NP)),
            dma((NP,)), dma((NP,)),
            dma((NZ,)), dma((NZ,)),
        ],
        compiler_params=pltpu.CompilerParams(
            collective_id=0, has_side_effects=True, vmem_limit_bytes=60 * 1024 * 1024
        ),
    )(
        queries,
        cache_keys.reshape(SEQ, CACHE, HD),
        cache_values.reshape(SEQ, CACHE, HD),
        new_keys.reshape(SEQ, STEPS, HD),
        new_values.reshape(SEQ, STEPS, HD),
        key_index, value_index, scale_table, lengths, head_mix, channel_mix, out_weight, residual.T,
    )
    return turned.T


def solution(mesh):
    in_specs = (
        P("dp", None, "head", None),
        P("dp", None, "head", None),
        P("dp", None, "head", None),
        P("dp", None, "head", None),
        P("dp", None, "head", None),
        P("head", None),
        P("head", None),
        P(),
        P("dp"),
        P(),
        P(),
        P("head", "dp"),
        P(None, ("dp", "head")),
    )
    out_specs = P(None, ("dp", "head"))
    return jax.shard_map(local, mesh=mesh, in_specs=in_specs, out_specs=out_specs, check_vma=False)
```
